1024 devices in a mesh: node: 16 (over z, core), local: 64 (over x, y).
Axes of the slice: x: 8, y: 8, z: 8, core: 2. Of those that a mesh axis runs over, the one named last changes fastest.
Arguments:
- out_grad: bfloat16 [8192, 7168], P('local', 'node'), may hold values from -0.796875 to 0.796875
- gate_weights: bfloat16 [8192, 8], P('local'), may hold values from 0.049804688 to 0.5
- expert_ids: int32 [8192, 8], P('local'), may hold values from 0 to 63, all different within a row; in each aligned block of 128 rows (0 to 127, 128 to 255, ...) at most 21 rows name the same one
- w_gate: bfloat16 [64, 7168, 1024], P('local', 'node'), may hold values from -0.1875 to 0.1875
- w_up: bfloat16 [64, 7168, 1024], P('local', 'node'), may hold values from -0.1875 to 0.1875
- w_down: bfloat16 [64, 1024, 7168], P('local', None, 'node'), may hold values from -0.0625 to 0.0625
- saved_gate: bfloat16 [64, 1024, 1344], P('local', 'node'), may hold values from -6 to 6
- saved_up: bfloat16 [64, 1024, 1344], P('local', 'node'), may hold values from -6 to 6
Outputs:
- input_grad: bfloat16 [8192, 7168], P('local', 'node')
- combine_grad: bfloat16 [8192, 8], P('local')
The draws below stay inside these ranges and needn't reach their ends.
Inputs may be any that keep to these rules, and one draw needn't show every extreme that they name: `expert_ids`: each row names 8 different experts; within the tokens of one index of local no expert is named by more than 21 rows, a bound that some block reaches.
All inputs are finite; a program needn't handle non-finite values.
Results may differ from the reference program's by a relative error of at most 0.0057.
Values may be sent and summed in bfloat16 or wider, within the bound.
No kernel may reach another device: no remote copies, remote signals or barrier semaphores. Data moves between devices by JAX's collectives and lax.ppermute only.
A program may use at most 64 MiB of HBM per device.

```python
import math
import jax
import jax.numpy as jnp
import numpy as np
from jax import lax

D = 7168
H = 1024
TOPK = 8
TOK = 128
EXPERTS = 64
CAP = 21
SLOTS = 1344
TOKENS = 8192
N_LOCAL = 64


def level_of(rng, shape, cuts, low, largest):
    factor_of, own = 1.0, jax.random.fold_in(rng, 6)
    for dim, parts in cuts:
        draws = jnp.exp(jax.random.uniform(jax.random.fold_in(own, dim), (parts,), jnp.float32, low / len(cuts), largest / len(cuts)))
        factor_of = factor_of * jnp.repeat(draws, shape[dim] // parts).reshape([-1 if axis == dim else 1 for axis in range(len(shape))])
    return factor_of


def shared_out(key, own, number, rows, amount, top, bound, skew):
    order = jax.random.permutation(key, amount)
    packed, ordinary = portions_of(amount, rows * top, bound, skew, True), portions_of(amount, rows * top, bound, skew, False)
    places = jnp.arange(amount)

    def named(lengths, offset_by):
        used = int((lengths > 0).sum())
        fixed = max(1, used // 4)
        shifted = fixed + (places - fixed + offset_by * (used - fixed)) % max(1, amount - fixed)
        return jnp.zeros((amount,), jnp.int32).at[order[jnp.where(places < fixed, places, shifted)]].set(jnp.asarray(lengths, jnp.int32))

    lengths = jnp.where(number % 4 == 0, named(packed, number // 4), named(ordinary, number - number // 4 - 1))
    mixed = jax.random.permutation(jax.random.fold_in(own, 3), amount)
    donor, sink = mixed[0:amount // 2 * 2:2], mixed[1:amount // 2 * 2:2]
    margin = jnp.minimum(lengths[donor] - 1, bound - lengths[sink]) // 2
    margin = jnp.where((donor == order[0]) | (sink == order[0]) | (lengths[sink] == 0), 0, jnp.maximum(margin, 0))
    shifted = jax.random.randint(jax.random.fold_in(own, 4), (amount // 2,), 0, 1 << 20) % (margin + 1)
    lengths = lengths.at[donor].add(-shifted).at[sink].add(shifted)
    labels = jnp.searchsorted(jnp.cumsum(lengths), jnp.arange(rows * top), side="right").astype(jnp.int32)
    table = labels.reshape(top, rows).T
    table = table[jax.random.permutation(jax.random.fold_in(own, 1), rows)]
    offset_by = jax.random.randint(jax.random.fold_in(own, 2), (rows, 1), 0, top)
    return jnp.take_along_axis(table, (jnp.arange(top)[None, :] + offset_by) % top, axis=1)


def portions_of(amount, total, bound, skew, full):
    weights = [(1 << 20) // math.isqrt(grade ** skew) + 1 for grade in range(1, amount + 1)]
    largest = bound if full else min(bound, max(-(-total // amount), total * weights[0] // sum(weights)))
    least = 1 if total - largest >= amount - 1 else 0
    counts, surplus = [largest] + [least] * (amount - 1), total - largest - least * (amount - 1)
    while surplus > 0:
        candidates = [i for i in range(1, amount) if counts[i] < largest] or [i for i in range(1, amount) if counts[i] < bound]
        whole, left = sum([weights[i] for i in candidates]), surplus
        for i in candidates:
            addition = min(bound - counts[i], max(1, left * weights[i] // whole), surplus)
            counts[i] = counts[i] + addition
            surplus = surplus - addition
    return np.array(counts)


def normal_values(key, extent, width, bound, pieces=(), kind=jnp.bfloat16):
    values = width * jax.random.normal(key, extent, jnp.float32)
    if pieces:
        values = values * level_of(key, extent, pieces, -0.22, 0.18)
    return jnp.clip(values, -bound, bound).astype(kind)


def setup_inputs(seed: int = 0) -> dict:
    key_list = jax.random.split(jax.random.key(seed), 9)
    out_grad = normal_values(key_list[0], (TOKENS, D), 0.1, 0.796875, ((0, 64), (1, 16)))
    gate_weights = jnp.clip(jnp.exp(math.log(0.5) - 2.306499 * jax.random.uniform(key_list[1], (TOKENS, TOPK), jnp.float32) ** level_of(key_list[1], (TOKENS, TOPK), ((0, 64),), -0.2, 0.2)), 0.049804688, 0.5).astype(jnp.bfloat16)
    expert_ids_keys = jax.random.split(jax.random.fold_in(key_list[2], 1), TOKENS // TOK)
    expert_ids_turns = jax.random.permutation(jax.random.fold_in(key_list[2], 3), TOKENS // TOK)
    expert_ids = jax.vmap(lambda own, number: shared_out(jax.random.fold_in(key_list[2], 2), own, number, TOK, EXPERTS, TOPK, CAP, 2))(expert_ids_keys, expert_ids_turns).reshape((TOKENS, TOPK))
    w_gate = normal_values(key_list[3], (EXPERTS, D, H), H ** -0.5, 0.1875, ((0, 64), (1, 16)))
    w_up = normal_values(key_list[4], (EXPERTS, D, H), H ** -0.5, 0.1875, ((0, 64), (1, 16)))
    w_down = normal_values(key_list[5], (EXPERTS, H, D), D ** -0.5, 0.0625, ((0, 64), (2, 16)))
    saved_gate = normal_values(key_list[6], (EXPERTS, H, SLOTS), 1.0, 6.0, ((0, 64), (1, 16)))
    saved_up = normal_values(key_list[7], (EXPERTS, H, SLOTS), 1.0, 6.0, ((0, 64), (1, 16)))
    return dict(out_grad=out_grad, gate_weights=gate_weights, expert_ids=expert_ids, w_gate=w_gate, w_up=w_up, w_down=w_down, saved_gate=saved_gate, saved_up=saved_up)


def slot_index(expert_ids):
    blocks = expert_ids.reshape(N_LOCAL, TOK * TOPK)
    onehot = (blocks[:, :, None] == jnp.arange(EXPERTS, dtype=jnp.int32)[None, None, :]).astype(jnp.int32)
    before = jnp.cumsum(onehot, axis=1) - onehot
    within = jnp.sum(before * onehot, axis=2).astype(jnp.int32)
    source = jnp.arange(N_LOCAL, dtype=jnp.int32)[:, None] * CAP
    flat = blocks * SLOTS + source + within
    return flat.reshape(-1).astype(jnp.int32)


def expert_backward(operands):
    received, slot_gate, gate_matrix, up_matrix, down_matrix, saved_g, saved_u = operands
    raw_grad = jnp.dot(received, down_matrix.T, preferred_element_type=jnp.float32)
    pre_gate = saved_g.T.astype(jnp.float32)
    pre_up = saved_u.T.astype(jnp.float32)
    sigma = jax.nn.sigmoid(pre_gate)
    activ = pre_gate * sigma
    slope = sigma * (1.0 + pre_gate * (1.0 - sigma))
    slot_combine = jnp.sum(raw_grad * activ * pre_up, axis=1)
    hidden_grad = raw_grad * slot_gate.astype(jnp.float32)[:, None]
    gate_pre = (hidden_grad * pre_up * slope).astype(jnp.bfloat16)
    up_pre = (hidden_grad * activ).astype(jnp.bfloat16)
    slot_input = jnp.dot(gate_pre, gate_matrix.T, preferred_element_type=jnp.float32)
    slot_input = slot_input + jnp.dot(up_pre, up_matrix.T, preferred_element_type=jnp.float32)
    return slot_input.astype(jnp.bfloat16), slot_combine.astype(jnp.bfloat16)


def reference(out_grad, gate_weights, expert_ids, w_gate, w_up, w_down, saved_gate, saved_up):
    flat = slot_index(expert_ids)
    repeated = jnp.repeat(out_grad, TOPK, axis=0)
    received = jnp.zeros((EXPERTS * SLOTS, D), jnp.bfloat16).at[flat].set(repeated).reshape(EXPERTS, SLOTS, D)
    slot_gate = jnp.zeros((EXPERTS * SLOTS,), jnp.bfloat16).at[flat].set(gate_weights.reshape(-1)).reshape(EXPERTS, SLOTS)
    slot_input, slot_combine = lax.map(expert_backward, (received, slot_gate, w_gate, w_up, w_down, saved_gate, saved_up))
    picked = slot_input.reshape(EXPERTS * SLOTS, D)[flat].reshape(TOKENS, TOPK, D).astype(jnp.float32)
    input_grad = jnp.sum(picked, axis=1).astype(jnp.bfloat16)
    combine_grad = slot_combine.reshape(-1)[flat].reshape(TOKENS, TOPK)
    return input_grad, combine_grad
```

```python
import jax
import jax.numpy as jnp
from jax import lax
from jax.experimental import pallas as pl
from jax.experimental.pallas import tpu as pltpu
from jax.sharding import PartitionSpec as P

BF = jnp.bfloat16
F32 = jnp.float32
PAD = 24
WIDE = 512
GROUP = 16
EXTRA = 16


def call(kernel, outs, *operands, smem=0, scratch=()):
    spec = [pl.BlockSpec(memory_space=pltpu.SMEM)] * smem
    spec += [pl.BlockSpec(memory_space=pltpu.VMEM)] * (len(operands) - smem)
    return pl.pallas_call(
        kernel,
        out_shape=outs,
        in_specs=spec,
        out_specs=jax.tree.map(lambda _: pl.BlockSpec(memory_space=pltpu.VMEM), outs),
        scratch_shapes=list(scratch),
        compiler_params=pltpu.CompilerParams(vmem_limit_bytes=48 * 2**20),
    )(*operands)


def dot(a, b, dims):
    return lax.dot_general(a, b, (dims, ((), ())), preferred_element_type=F32)


NN = ((1,), (0,))
NT = ((1,), (1,))


def one_hot_rows(rank, experts, tokens):
    place = lax.broadcasted_iota(jnp.int32, (experts, PAD, tokens), 1).astype(F32)
    return jnp.where(rank[:, None, :] == place, 1.0, 0.0).astype(F32)


def packing(capacity, wide_first):
    tight, wide = GROUP * capacity, GROUP * PAD
    shape = (wide, tight) if wide_first else (tight, wide)
    r = lax.broadcasted_iota(jnp.int32, shape, 1 if wide_first else 0)
    q = lax.broadcasted_iota(jnp.int32, shape, 0 if wide_first else 1)
    source = jnp.zeros(shape, jnp.int32)
    for s in range(1, GROUP):
        source += jnp.where(r >= s * capacity, 1, 0)
    return jnp.where(q == r + source * (PAD - capacity), 1.0, 0.0).astype(BF)


def dispatch_kernel(ids_ref, gates_ref, grad_ref, send_ref, rank_ref):
    experts, tokens = rank_ref.shape
    expert = lax.broadcasted_iota(jnp.int32, (experts, tokens), 0)
    mask = jnp.zeros((experts, tokens), F32)
    weight = jnp.zeros((experts, tokens), F32)
    for k in range(ids_ref.shape[0]):
        hit = ids_ref[k : k + 1, :] == expert
        mask = jnp.where(hit, 1.0, mask)
        weight = jnp.where(hit, gates_ref[k : k + 1, :].astype(F32), weight)
    earlier = lax.broadcasted_iota(jnp.int32, (tokens, tokens), 0) < lax.broadcasted_iota(
        jnp.int32, (tokens, tokens), 1
    )
    rank = dot(mask.astype(BF), jnp.where(earlier, 1.0, 0.0).astype(BF), NN)
    rank = jnp.where(mask > 0.0, rank, -1.0)
    rank_ref[...] = rank
    pick = one_hot_rows(rank, experts, tokens)
    gate = jnp.sum(pick * weight[:, None, :], axis=2, keepdims=True)
    features = grad_ref.shape[0]
    flat = pick.reshape(experts * PAD, tokens).astype(BF)
    send_ref[:, :features] = dot(flat, grad_ref[...], NT).astype(BF)
    send_ref[:, features:] = jnp.broadcast_to(
        gate.reshape(experts * PAD, 1), (experts * PAD, WIDE - features)
    ).astype(BF)


def weights_kernel(core_ref, own_ref, other_ref, out_ref):
    core = core_ref[0]
    features, hidden = own_ref.shape
    half = hidden // 2
    for i, ref in enumerate((own_ref, other_ref)):
        rows = ref[...].astype(F32).T.reshape(hidden // 128, 128, features)
        rows = jnp.where(core == 0, rows[:, :64], rows[:, 64:])
        out_ref[i] = rows.reshape(half, features).astype(BF)


def sum_features_kernel(own_ref, other_ref, weight_ref, out_ref, gate_ref, rows_ref):
    features = weight_ref.shape[2]
    slots = out_ref.shape[1]
    groups = own_ref.shape[0] // (GROUP * PAD)
    tight, wide = slots // groups, GROUP * PAD
    pack = packing(tight // GROUP, False)
    for i, ref in enumerate((own_ref, other_ref)):
        for g in range(groups):
            rows_ref[i, g * tight : (g + 1) * tight, :] = dot(
                pack, ref[g * wide : (g + 1) * wide, :], NN
            ).astype(BF)
    total = dot(weight_ref[0], rows_ref[0, :, :features], NT)
    total += dot(weight_ref[1], rows_ref[1, :, :features], NT)
    out_ref[...] = total.astype(BF)
    lane = lax.broadcasted_iota(jnp.int32, (8, 128), 1)
    at = jnp.where(lane == features % 128, 1.0, 0.0).astype(BF)
    gate_ref[...] = dot(at, rows_ref[0, :, WIDE - 128 :], NT)


def hidden_kernel(parts_ref, gate_ref, up_ref, slot_gate_ref, out_ref):
    raw = parts_ref[0].astype(F32)
    for i in range(1, parts_ref.shape[0]):
        raw += parts_ref[i].astype(F32)
    g = gate_ref[...].astype(F32)
    u = up_ref[...].astype(F32)
    sigma = 1.0 / (1.0 + jnp.exp(-g))
    activ = g * sigma
    slope = sigma * (1.0 + g * (1.0 - sigma))
    combine = jnp.sum(raw * activ * u, axis=0, keepdims=True)
    scaled = raw * slot_gate_ref[0:1, :]
    units = g.shape[0]
    out_ref[:units, :] = (scaled * u * slope).astype(BF)
    out_ref[units : 2 * units, :] = (scaled * activ).astype(BF)
    high = combine.astype(BF).astype(F32)
    row = lax.broadcasted_iota(jnp.int32, (EXTRA, g.shape[1]), 0)
    extra = jnp.where(row == 0, high, jnp.where(row == 1, combine - high, 0.0))
    out_ref[2 * units :, :] = extra.astype(BF)


def input_kernel(all_ref, gate_ref, up_ref, out_ref, wide_ref, rows_ref):
    nodes, height, slots = all_ref.shape
    units = (height - EXTRA) // 2
    features = gate_ref.shape[0]
    gate_pre = all_ref[:, :units, :].reshape(nodes * units, slots)
    up_pre = all_ref[:, units : 2 * units, :].reshape(nodes * units, slots)
    wide_ref[:features, :slots] = dot(gate_ref[...], gate_pre, NN) + dot(up_ref[...], up_pre, NN)
    extra = all_ref[0, 2 * units :, :].astype(F32)
    for n in range(1, nodes):
        extra += all_ref[n, 2 * units :, :].astype(F32)
    wide_ref[features:, :slots] = jnp.broadcast_to(
        extra[0:1] + extra[1:2], (WIDE - features, slots)
    )
    spare = wide_ref.shape[1] - slots
    if spare:
        wide_ref[:, slots:] = jnp.zeros((WIDE, spare), F32)
    rows_ref[...] = wide_ref[...].T.astype(BF)
    groups = out_ref.shape[0] // (GROUP * PAD)
    tight, wide = slots // groups, GROUP * PAD
    unpack = packing(tight // GROUP, True)
    for g in range(groups):
        out_ref[g * wide : (g + 1) * wide, :] = dot(
            unpack, rows_ref[g * tight : (g + 1) * tight, :], NN
        ).astype(BF)


def collect_kernel(back_ref, rank_ref, ids_ref, grad_ref, combine_ref):
    experts, tokens = rank_ref.shape
    features = grad_ref.shape[0]
    pick = one_hot_rows(rank_ref[...], experts, tokens)
    turned = back_ref[...].astype(F32).T.astype(BF)
    flat = pick.reshape(experts * PAD, tokens).astype(BF)
    grad_ref[...] = dot(turned, flat, NN)[:features].astype(BF)
    column = back_ref[:, WIDE - 128 :].astype(F32)[:, features % 128 : features % 128 + 1]
    chosen = jnp.sum(pick * column.reshape(experts, PAD, 1), axis=1)
    expert = lax.broadcasted_iota(jnp.int32, (experts, tokens), 0)
    for k in range(ids_ref.shape[0]):
        hit = ids_ref[k : k + 1, :] == expert
        combine_ref[k : k + 1, :] = jnp.sum(jnp.where(hit, chosen, 0.0), axis=0, keepdims=True)


def body(out_grad, gate_weights, expert_ids, w_gate, w_up, w_down, saved_gate, saved_up):
    experts = lax.axis_size("local")
    nodes = lax.axis_size("node")
    tokens, features = out_grad.shape
    top = expert_ids.shape[1]
    units, slots = saved_gate.shape[1:]
    hidden = w_down.shape[1]
    shape = jax.ShapeDtypeStruct
    swap = [(i, i ^ 1) for i in range(nodes)]
    columns = [list(range(core, nodes, 2)) for core in range(2)]

    ids = expert_ids.T
    send, rank = call(
        dispatch_kernel,
        (shape((experts * PAD, WIDE), BF), shape((experts, tokens), F32)),
        ids,
        gate_weights.T,
        out_grad.T,
    )
    arrived = lax.all_to_all(
        send.reshape(experts, PAD, WIDE), "local", split_axis=0, concat_axis=0, tiled=True
    )
    down = w_down[0].T
    core = (lax.axis_index("node") % 2).astype(jnp.int32).reshape(1)
    weights = call(
        weights_kernel,
        shape((2, hidden // 2, features), BF),
        core,
        down,
        lax.ppermute(down, "node", swap),
        smem=1,
    )
    partner = lax.ppermute(arrived, "node", swap)
    partial, slot_gate = call(
        sum_features_kernel,
        (shape((hidden // 2, slots), BF), shape((8, slots), F32)),
        arrived.reshape(experts * PAD, WIDE),
        partner.reshape(experts * PAD, WIDE),
        weights,
        scratch=[pltpu.VMEM((2, slots, WIDE), BF)],
    )
    parts = lax.all_to_all(
        partial.reshape(nodes // 2, units, slots),
        "node",
        split_axis=0,
        concat_axis=0,
        tiled=True,
        axis_index_groups=columns,
    )
    piece = call(
        hidden_kernel,
        shape((2 * units + EXTRA, slots), BF),
        parts,
        saved_gate[0],
        saved_up[0],
        slot_gate,
    )
    gathered = lax.all_gather(piece, "node", axis=0, tiled=False)
    rounded = -(-slots // 128) * 128
    back = call(
        input_kernel,
        shape((experts * PAD, WIDE), BF),
        gathered,
        w_gate[0],
        w_up[0],
        scratch=[pltpu.VMEM((WIDE, rounded), F32), pltpu.VMEM((rounded, WIDE), BF)],
    )
    returned = lax.all_to_all(
        back.reshape(experts, PAD, WIDE), "local", split_axis=0, concat_axis=0, tiled=True
    )
    grad, combine = call(
        collect_kernel,
        (shape((features, tokens), BF), shape((top, tokens), F32)),
        returned.reshape(experts * PAD, WIDE),
        rank,
        ids,
    )
    return grad.T, combine.T.astype(BF)


def solution(mesh):
    in_specs = (
        P("local", "node"),
        P("local", None),
        P("local", None),
        P("local", "node", None),
        P("local", "node", None),
        P("local", None, "node"),
        P("local", "node", None),
        P("local", "node", None),
    )
    out_specs = (P("local", "node"), P("local", None))
    return jax.shard_map(body, mesh=mesh, in_specs=in_specs, out_specs=out_specs, check_vma=False)
```

```python
import functools

import jax
import jax.numpy as jnp
from jax import lax
from jax.experimental import pallas as pl
from jax.experimental.pallas import tpu as pltpu
from jax.sharding import PartitionSpec as P

BF = jnp.bfloat16
F32 = jnp.float32
LANES = 128
GROUP = 8
EXTRA = 16


def call(kernel, outs, *operands, smem=0, scratch=()):
    spec = [pl.BlockSpec(memory_space=pltpu.SMEM)] * smem
    spec += [pl.BlockSpec(memory_space=pltpu.VMEM)] * (len(operands) - smem)
    return pl.pallas_call(
        kernel,
        out_shape=outs,
        in_specs=spec,
        out_specs=jax.tree.map(lambda _: pl.BlockSpec(memory_space=pltpu.VMEM), outs),
        scratch_shapes=list(scratch),
        compiler_params=pltpu.CompilerParams(vmem_limit_bytes=48 * 2**20),
    )(*operands)


def dot(a, b, dims):
    return lax.dot_general(a, b, (dims, ((), ())), preferred_element_type=F32)


NN = ((1,), (0,))
NT = ((1,), (1,))


def layout(features, capacity):
    full = features // LANES
    scalars = full * capacity + (capacity + 1) // 2
    return full, scalars, -(-(scalars + 1) // 16) * 16


def place_codes(features, capacity):
    full, scalars, rows = layout(features, capacity)
    q = lax.broadcasted_iota(jnp.int32, (rows, LANES), 0)
    codes = []
    for c in range(full):
        at = q - c * capacity
        codes.append(jnp.where((at >= 0) & (at < capacity), at, -2))
    at = 2 * (q - full * capacity)
    tail = (at >= 0) & (q < scalars)
    codes.append(jnp.where(tail, at, -2))
    codes.append(jnp.where(tail & (at + 1 < capacity), at + 1, -2))
    return [code.astype(F32).astype(BF) for code in codes]


def picks(rank, features, capacity):
    experts, tokens = rank.shape
    one, zero = jnp.ones((), BF), jnp.zeros((), BF)
    place = rank.astype(BF)[:, None, :]
    out = []
    for code in place_codes(features, capacity):
        hit = jnp.where(place == code[None], one, zero)
        out.append(hit.reshape(experts * code.shape[0], tokens))
    return out


def slot_diagonal(height):
    j = lax.broadcasted_iota(jnp.int32, (1, height, LANES), 1)
    lane = lax.broadcasted_iota(jnp.int32, (1, height, LANES), 2)
    return jnp.where(j == lane, 1.0, 0.0).astype(F32)


def slot_of_row(shape, dim, capacity):
    r = lax.broadcasted_iota(jnp.int32, shape, dim)
    source = jnp.zeros(shape, jnp.int32)
    for s in range(1, GROUP):
        source += jnp.where(r >= s * capacity, 1, 0)
    return source, r - source * capacity


def packing(features, capacity, rows_first):
    full, scalars, rows = layout(features, capacity)
    tight, wide = GROUP * capacity, GROUP * rows
    shape = (wide, tight) if rows_first else (tight, wide)
    source, slot = slot_of_row(shape, 1 if rows_first else 0, capacity)
    at = lax.broadcasted_iota(jnp.int32, shape, 0 if rows_first else 1) - source * rows
    targets = [slot + c * capacity for c in range(full)]
    targets += [lax.shift_right_logical(slot, 1) + full * capacity, scalars]
    return [jnp.where(at == target, 1.0, 0.0).astype(BF) for target in targets]


def odd(slot):
    return (slot & 1) == 1


def dispatch_kernel(capacity, ids_ref, gates_ref, grad_ref, send_ref, rank_ref):
    experts, tokens = rank_ref.shape
    features = grad_ref.shape[0]
    full, scalars, rows = layout(features, capacity)
    expert = lax.broadcasted_iota(jnp.int32, (experts, tokens), 0)
    mask = jnp.zeros((experts, tokens), F32)
    weight = jnp.zeros((experts, tokens), F32)
    for k in range(ids_ref.shape[0]):
        hit = ids_ref[k : k + 1, :] == expert
        mask = jnp.where(hit, 1.0, mask)
        weight = jnp.where(hit, gates_ref[k : k + 1, :].astype(F32), weight)
    earlier = lax.broadcasted_iota(jnp.int32, (tokens, tokens), 0) < lax.broadcasted_iota(
        jnp.int32, (tokens, tokens), 1
    )
    rank = dot(mask.astype(BF), jnp.where(earlier, 1.0, 0.0).astype(BF), NN)
    rank = jnp.where(mask > 0.0, rank, -1.0)
    rank_ref[...] = rank
    height = -(-capacity // 8) * 8
    j = lax.broadcasted_iota(jnp.int32, (experts, height, tokens), 1).astype(F32)
    gate = jnp.where(rank[:, None, :] == j, weight[:, None, :], 0.0)
    gate = jnp.sum(gate, axis=2, keepdims=True)
    gate = jnp.sum(gate * slot_diagonal(height), axis=1, keepdims=True)
    tail = grad_ref[full * LANES :, :]
    empty = jnp.zeros((LANES - tail.shape[0], tokens), BF)
    pieces = [grad_ref[c * LANES : (c + 1) * LANES, :] for c in range(full)]
    pieces += [jnp.concatenate([tail, empty], axis=0), jnp.concatenate([empty, tail], axis=0)]
    total = jnp.zeros((experts * rows, LANES), F32)
    for pick, piece in zip(picks(rank, features, capacity), pieces):
        total += dot(pick, piece, NT)
    q = lax.broadcasted_iota(jnp.int32, (experts, rows, LANES), 1)
    total = jnp.where(q == scalars, gate, total.reshape(experts, rows, LANES))
    send_ref[...] = total.reshape(experts * rows, LANES).astype(BF)


def weights_kernel(core_ref, down_ref, out_ref):
    core = core_ref[0]
    features, hidden = down_ref.shape
    half = hidden // 2
    rows = down_ref[...].astype(F32).T.reshape(hidden // LANES, LANES, features)
    low, high = rows[:, :64], rows[:, 64:]
    out_ref[0] = jnp.where(core == 0, low, high).reshape(half, features).astype(BF)
    out_ref[1] = jnp.where(core == 0, high, low).reshape(half, features).astype(BF)


def other_half_kernel(capacity, arrived_ref, weight_ref, out_ref, rows_ref, gate_ref):
    features = weight_ref.shape[2]
    full, _, rows = layout(features, capacity)
    tight, wide = GROUP * capacity, GROUP * rows
    groups = arrived_ref.shape[0] // wide
    packs = packing(features, capacity, False)
    _, slot = slot_of_row((tight, LANES), 0, capacity)
    lane = lax.broadcasted_iota(jnp.int32, (tight, LANES), 1)
    for g in range(0, groups, 2):
        pair = jnp.concatenate(
            [arrived_ref[h * wide : (h + 1) * wide, :] for h in (g, g + 1)], axis=1
        )
        at = slice(g * tight, (g + 2) * tight)
        got = [dot(pack, pair, NN) for pack in packs]
        for c in range(full + 1):
            halves = []
            for h in range(2):
                piece = got[c][:, h * LANES : (h + 1) * LANES]
                if c == full:
                    gates = got[full + 1][:, h * LANES : (h + 1) * LANES]
                    gate = jnp.sum(jnp.where(lane == slot, gates, 0.0), axis=1, keepdims=True)
                    piece = jnp.where(odd(slot), pltpu.roll(piece, 64, 1), piece)
                    piece = jnp.where(lane < 64, piece, gate)
                halves.append(piece)
            rows_ref[at, c * LANES : (c + 1) * LANES] = jnp.concatenate(halves, axis=0).astype(BF)
    out_ref[...] = dot(weight_ref[1], rows_ref[:, :features], NT).astype(BF)
    lane = lax.broadcasted_iota(jnp.int32, (8, LANES), 1)
    at = jnp.where(lane == 64, 1.0, 0.0).astype(BF)
    gate_ref[...] = dot(at, rows_ref[:, full * LANES :], NT)


def own_half_kernel(rows_ref, weight_ref, partner_ref, out_ref):
    features = weight_ref.shape[2]
    total = dot(weight_ref[0], rows_ref[:, :features], NT)
    out_ref[...] = (total + partner_ref[...].astype(F32)).astype(BF)


def hidden_kernel(parts_ref, gate_ref, up_ref, slot_gate_ref, out_ref):
    raw = parts_ref[0].astype(F32)
    for i in range(1, parts_ref.shape[0]):
        raw += parts_ref[i].astype(F32)
    g = gate_ref[...].astype(F32)
    u = up_ref[...].astype(F32)
    sigma = 1.0 / (1.0 + jnp.exp(-g))
    activ = g * sigma
    slope = sigma * (1.0 + g * (1.0 - sigma))
    combine = jnp.sum(raw * activ * u, axis=0, keepdims=True)
    scaled = raw * slot_gate_ref[0:1, :]
    units = g.shape[0]
    out_ref[:units, :] = (scaled * u * slope).astype(BF)
    out_ref[units : 2 * units, :] = (scaled * activ).astype(BF)
    high = combine.astype(BF).astype(F32)
    row = lax.broadcasted_iota(jnp.int32, (EXTRA, g.shape[1]), 0)
    extra = jnp.where(row == 0, high, jnp.where(row == 1, combine - high, 0.0))
    out_ref[2 * units :, :] = extra.astype(BF)


def input_kernel(capacity, all_ref, gate_ref, up_ref, out_ref, wide_ref, rows_ref):
    nodes, height, slots = all_ref.shape
    units = (height - EXTRA) // 2
    features = gate_ref.shape[0]
    gate_pre = all_ref[:, :units, :].reshape(nodes * units, slots)
    up_pre = all_ref[:, units : 2 * units, :].reshape(nodes * units, slots)
    wide_ref[:features, :slots] = dot(gate_ref[...], gate_pre, NN) + dot(up_ref[...], up_pre, NN)
    extra = all_ref[0, 2 * units :, :].astype(F32)
    for n in range(1, nodes):
        extra += all_ref[n, 2 * units :, :].astype(F32)
    spare = wide_ref.shape[0] - features
    wide_ref[features:, :slots] = jnp.broadcast_to(extra[0:1] + extra[1:2], (spare, slots))
    beyond = wide_ref.shape[1] - slots
    if beyond:
        wide_ref[:, slots:] = jnp.zeros((wide_ref.shape[0], beyond), F32)
    rows_ref[...] = wide_ref[...].T
    full, _, rows = layout(features, capacity)
    tight, wide = GROUP * capacity, GROUP * rows
    groups = slots // tight
    packs = packing(features, capacity, True)
    _, slot = slot_of_row((tight, LANES), 0, capacity)
    lane = lax.broadcasted_iota(jnp.int32, (tight, LANES), 1)
    for g in range(0, groups, 2):
        pieces = []
        for h in (g, g + 1):
            at = slice(h * tight, (h + 1) * tight)
            mine = [rows_ref[at, c * LANES : (c + 1) * LANES] for c in range(full + 1)]
            tail = mine.pop()
            turned = pltpu.roll(tail, 64, 1)
            mine.append(jnp.where((lane >= 64) == odd(slot), jnp.where(odd(slot), turned, tail), 0.0))
            scalar = jnp.where(lane < 64, turned, tail)
            mine.append(jnp.where(lane == slot, scalar, 0.0))
            pieces.append([piece.astype(BF) for piece in mine])
        total = jnp.zeros((wide, 2 * LANES), F32)
        for pack, low, high in zip(packs, *pieces):
            total += dot(pack, jnp.concatenate([low, high], axis=1), NN)
        for h in range(2):
            out_ref[(g + h) * wide : (g + h + 1) * wide, :] = total[
                :, h * LANES : (h + 1) * LANES
            ].astype(BF)


def collect_kernel(capacity, back_ref, rank_ref, ids_ref, grad_ref, combine_ref):
    experts, tokens = rank_ref.shape
    features = grad_ref.shape[0]
    full, scalars, rows = layout(features, capacity)
    rank = rank_ref[...]
    values = back_ref[...].astype(F32)
    turned = values.T.astype(BF)
    sums = [dot(turned, pick, NN) for pick in picks(rank, features, capacity)]
    for c in range(full):
        grad_ref[c * LANES : (c + 1) * LANES, :] = sums[c].astype(BF)
    grad_ref[full * LANES :, :] = (sums[full][:64] + sums[full + 1][64:]).astype(BF)
    height = -(-capacity // 8) * 8
    carried = values.reshape(experts, rows, LANES)[:, scalars : scalars + 1, :]
    column = jnp.sum(carried * slot_diagonal(height), axis=2, keepdims=True)
    j = lax.broadcasted_iota(jnp.int32, (experts, height, tokens), 1).astype(F32)
    chosen = jnp.sum(jnp.where(rank[:, None, :] == j, column, 0.0), axis=1)
    expert = lax.broadcasted_iota(jnp.int32, (experts, tokens), 0)
    for k in range(ids_ref.shape[0]):
        hit = ids_ref[k : k + 1, :] == expert
        combine_ref[k : k + 1, :] = jnp.sum(jnp.where(hit, chosen, 0.0), axis=0, keepdims=True)


def body(out_grad, gate_weights, expert_ids, w_gate, w_up, w_down, saved_gate, saved_up):
    experts = lax.axis_size("local")
    nodes = lax.axis_size("node")
    tokens, features = out_grad.shape
    top = expert_ids.shape[1]
    units, slots = saved_gate.shape[1:]
    hidden = w_down.shape[1]
    shape = jax.ShapeDtypeStruct
    swap = [(i, i ^ 1) for i in range(nodes)]
    columns = [list(range(core, nodes, 2)) for core in range(2)]

    capacity = slots // experts
    rows = layout(features, capacity)[2]
    lanes = -(-features // LANES) * LANES
    ids = expert_ids.T
    send, rank = call(
        functools.partial(dispatch_kernel, capacity),
        (shape((experts * rows, LANES), BF), shape((experts, tokens), F32)),
        ids,
        gate_weights.T,
        out_grad.T,
    )
    arrived = lax.all_to_all(
        send.reshape(experts, rows, LANES), "local", split_axis=0, concat_axis=0, tiled=True
    )
    core = (lax.axis_index("node") % 2).astype(jnp.int32).reshape(1)
    weights = call(
        weights_kernel, shape((2, hidden // 2, features), BF), core, w_down[0].T, smem=1
    )
    other, packed, slot_gate = call(
        functools.partial(other_half_kernel, capacity),
        (shape((hidden // 2, slots), BF), shape((slots, lanes), BF), shape((8, slots), F32)),
        arrived.reshape(experts * rows, LANES),
        weights,
    )
    partial = call(
        own_half_kernel,
        shape((hidden // 2, slots), BF),
        packed,
        weights,
        lax.ppermute(other, "node", swap),
    )
    parts = lax.all_to_all(
        partial.reshape(nodes // 2, units, slots),
        "node",
        split_axis=0,
        concat_axis=0,
        tiled=True,
        axis_index_groups=columns,
    )
    piece = call(
        hidden_kernel,
        shape((2 * units + EXTRA, slots), BF),
        parts,
        saved_gate[0],
        saved_up[0],
        slot_gate,
    )
    gathered = lax.all_gather(piece, "node", axis=0, tiled=False)
    rounded = -(-slots // 128) * 128
    back = call(
        functools.partial(input_kernel, capacity),
        shape((experts * rows, LANES), BF),
        gathered,
        w_gate[0],
        w_up[0],
        scratch=[pltpu.VMEM((lanes, rounded), F32), pltpu.VMEM((rounded, lanes), F32)],
    )
    returned = lax.all_to_all(
        back.reshape(experts, rows, LANES), "local", split_axis=0, concat_axis=0, tiled=True
    )
    grad, combine = call(
        functools.partial(collect_kernel, capacity),
        (shape((features, tokens), BF), shape((top, tokens), F32)),
        returned.reshape(experts * rows, LANES),
        rank,
        ids,
    )
    return grad.T, combine.T.astype(BF)


def solution(mesh):
    in_specs = (
        P("local", "node"),
        P("local", None),
        P("local", None),
        P("local", "node", None),
        P("local", "node", None),
        P("local", None, "node"),
        P("local", "node", None),
        P("local", "node", None),
    )
    out_specs = (P("local", "node"), P("local", None))
    return jax.shard_map(body, mesh=mesh, in_specs=in_specs, out_specs=out_specs, check_vma=False)
```

```python
import functools

import jax
import jax.numpy as jnp
from jax import lax
from jax.experimental import pallas as pl
from jax.experimental.pallas import tpu as pltpu
from jax.sharding import PartitionSpec as P

BF = jnp.bfloat16
F32 = jnp.float32
LANES = 128
GROUP = 8
EXTRA = 16


def call(kernel, outs, *operands, smem=0, scratch=(), plain=False):
    vmem = pl.BlockSpec() if plain else pl.BlockSpec(memory_space=pltpu.VMEM)
    spec = [pl.BlockSpec(memory_space=pltpu.SMEM)] * smem
    spec += [vmem] * (len(operands) - smem)
    return pl.pallas_call(
        kernel,
        out_shape=outs,
        in_specs=spec,
        out_specs=jax.tree.map(lambda _: vmem, outs),
        scratch_shapes=list(scratch),
        compiler_params=pltpu.CompilerParams(vmem_limit_bytes=32 * 2**20),
    )(*operands)


def dot(a, b, dims):
    return lax.dot_general(a, b, (dims, ((), ())), preferred_element_type=F32)


NN = ((1,), (0,))
NT = ((1,), (1,))


def layout(features, capacity):
    full = features // LANES
    scalars = full * capacity + (capacity + 1) // 2
    return full, scalars, -(-(scalars + 1) // 16) * 16


def place_codes(features, capacity):
    full, scalars, rows = layout(features, capacity)
    q = lax.broadcasted_iota(jnp.int32, (rows, LANES), 0)
    codes = []
    for c in range(full):
        at = q - c * capacity
        codes.append(jnp.where((at >= 0) & (at < capacity), at, -2))
    at = 2 * (q - full * capacity)
    tail = (at >= 0) & (q < scalars)
    codes.append(jnp.where(tail, at, -2))
    codes.append(jnp.where(tail & (at + 1 < capacity), at + 1, -2))
    return [code.astype(F32).astype(BF) for code in codes]


def picks(rank, features, capacity):
    experts, tokens = rank.shape
    one, zero = jnp.ones((), BF), jnp.zeros((), BF)
    place = rank.astype(BF)[:, None, :]
    out = []
    for code in place_codes(features, capacity):
        hit = jnp.where(place == code[None], one, zero)
        out.append(hit.reshape(experts * code.shape[0], tokens))
    return out


def slot_diagonal(height):
    j = lax.broadcasted_iota(jnp.int32, (1, height, LANES), 1)
    lane = lax.broadcasted_iota(jnp.int32, (1, height, LANES), 2)
    return jnp.where(j == lane, 1.0, 0.0).astype(F32)


def slot_of_row(shape, dim, capacity):
    r = lax.broadcasted_iota(jnp.int32, shape, dim)
    source = jnp.zeros(shape, jnp.int32)
    for s in range(1, GROUP):
        source += jnp.where(r >= s * capacity, 1, 0)
    return source, r - source * capacity


def packing(features, capacity, rows_first):
    full, scalars, rows = layout(features, capacity)
    tight, wide = GROUP * capacity, GROUP * rows
    shape = (wide, tight) if rows_first else (tight, wide)
    source, slot = slot_of_row(shape, 1 if rows_first else 0, capacity)
    at = lax.broadcasted_iota(jnp.int32, shape, 0 if rows_first else 1) - source * rows
    targets = [slot + c * capacity for c in range(full)]
    targets += [lax.shift_right_logical(slot, 1) + full * capacity, scalars]
    return [jnp.where(at == target, 1.0, 0.0).astype(BF) for target in targets]


def odd(slot):
    return (slot & 1) == 1


def dispatch_kernel(capacity, ids_ref, gates_ref, grad_ref, send_ref, rank_ref):
    experts, tokens = rank_ref.shape
    features = grad_ref.shape[0]
    full, scalars, rows = layout(features, capacity)
    expert = lax.broadcasted_iota(jnp.int32, (experts, tokens), 0)
    mask = jnp.zeros((experts, tokens), F32)
    weight = jnp.zeros((experts, tokens), F32)
    for k in range(ids_ref.shape[0]):
        hit = ids_ref[k : k + 1, :] == expert
        mask = jnp.where(hit, 1.0, mask)
        weight = jnp.where(hit, gates_ref[k : k + 1, :].astype(F32), weight)
    earlier = lax.broadcasted_iota(jnp.int32, (tokens, tokens), 0) < lax.broadcasted_iota(
        jnp.int32, (tokens, tokens), 1
    )
    rank = dot(mask.astype(BF), jnp.where(earlier, 1.0, 0.0).astype(BF), NN)
    rank = jnp.where(mask > 0.0, rank, -1.0)
    rank_ref[...] = rank
    height = -(-capacity // 8) * 8
    j = lax.broadcasted_iota(jnp.int32, (experts, height, tokens), 1).astype(F32)
    gate = jnp.where(rank[:, None, :] == j, weight[:, None, :], 0.0)
    gate = jnp.sum(gate, axis=2, keepdims=True)
    gate = jnp.sum(gate * slot_diagonal(height), axis=1, keepdims=True)
    tail = grad_ref[full * LANES :, :]
    empty = jnp.zeros((LANES - tail.shape[0], tokens), BF)
    pieces = [grad_ref[c * LANES : (c + 1) * LANES, :] for c in range(full)]
    pieces += [jnp.concatenate([tail, empty], axis=0), jnp.concatenate([empty, tail], axis=0)]
    total = jnp.zeros((experts * rows, LANES), F32)
    for pick, piece in zip(picks(rank, features, capacity), pieces):
        total += dot(pick, piece, NT)
    q = lax.broadcasted_iota(jnp.int32, (experts, rows, LANES), 1)
    total = jnp.where(q == scalars, gate, total.reshape(experts, rows, LANES))
    send_ref[...] = total.reshape(experts * rows, LANES).astype(BF)


def weights_kernel(place_ref, down_ref, out_ref, rows_ref):
    core, start = place_ref[0], place_ref[1]
    features, hidden = down_ref.shape
    blocks = hidden // LANES
    rows = down_ref[...].astype(F32).T.reshape(blocks, LANES, features)
    low, high = rows[:, :64], rows[:, 64:]
    rows_ref[0] = jnp.where(core == 0, low, high)
    rows_ref[1] = jnp.where(core == 0, high, low)
    for step in range(blocks):
        block = lax.rem(start + step, blocks)
        for half in range(2):
            out_ref[half, step * 64 : (step + 1) * 64, :] = rows_ref[half, block].astype(BF)


def other_half_kernel(capacity, arrived_ref, weight_ref, out_ref, rows_ref, gate_ref):
    features = weight_ref.shape[2]
    full, _, rows = layout(features, capacity)
    tight, wide = GROUP * capacity, GROUP * rows
    groups = arrived_ref.shape[0] // wide
    packs = packing(features, capacity, False)
    _, slot = slot_of_row((tight, LANES), 0, capacity)
    lane = lax.broadcasted_iota(jnp.int32, (tight, LANES), 1)
    for g in range(0, groups, 2):
        pair = jnp.concatenate(
            [arrived_ref[h * wide : (h + 1) * wide, :] for h in (g, g + 1)], axis=1
        )
        at = slice(g * tight, (g + 2) * tight)
        got = [dot(pack, pair, NN) for pack in packs]
        for c in range(full + 1):
            halves = []
            for h in range(2):
                piece = got[c][:, h * LANES : (h + 1) * LANES]
                if c == full:
                    gates = got[full + 1][:, h * LANES : (h + 1) * LANES]
                    gate = jnp.sum(jnp.where(lane == slot, gates, 0.0), axis=1, keepdims=True)
                    piece = jnp.where(odd(slot), pltpu.roll(piece, 64, 1), piece)
                    piece = jnp.where(lane < 64, piece, gate)
                halves.append(piece)
            rows_ref[at, c * LANES : (c + 1) * LANES] = jnp.concatenate(halves, axis=0).astype(BF)
    slots = rows_ref.shape[0]
    out_ref[:, :slots] = dot(weight_ref[1], rows_ref[:, :features], NT).astype(BF)
    if out_ref.shape[1] > slots:
        out_ref[:, slots:] = jnp.zeros((out_ref.shape[0], out_ref.shape[1] - slots), BF)
    lane = lax.broadcasted_iota(jnp.int32, (8, LANES), 1)
    at = jnp.where(lane == 64, 1.0, 0.0).astype(BF)
    gate_ref[...] = dot(at, rows_ref[:, full * LANES :], NT)


def own_half_kernel(rows_ref, weight_ref, partner_ref, *out_refs):
    features = weight_ref.shape[2]
    slots = rows_ref.shape[0]
    units = out_refs[0].shape[0]
    total = dot(weight_ref[0], rows_ref[:, :features], NT) + partner_ref[:, :slots].astype(F32)
    for step, out_ref in enumerate(out_refs):
        out_ref[:, :slots] = total[step * units : (step + 1) * units].astype(out_ref.dtype)
        if out_ref.shape[1] > slots:
            out_ref[:, slots:] = jnp.zeros((units, out_ref.shape[1] - slots), out_ref.dtype)


def hidden_kernel(gate_ref, up_ref, slot_gate_ref, *refs):
    *parts, out_ref = refs
    slots = gate_ref.shape[1]
    raw = parts[0][:, :slots].astype(F32)
    for part in parts[1:]:
        raw += part[:, :slots].astype(F32)
    g = gate_ref[...].astype(F32)
    u = up_ref[...].astype(F32)
    sigma = 1.0 / (1.0 + jnp.exp(-g))
    activ = g * sigma
    slope = sigma * (1.0 + g * (1.0 - sigma))
    combine = jnp.sum(raw * activ * u, axis=0, keepdims=True)
    scaled = raw * slot_gate_ref[0:1, :]
    units = g.shape[0]
    out_ref[:units, :] = (scaled * u * slope).astype(BF)
    out_ref[units : 2 * units, :] = (scaled * activ).astype(BF)
    high = combine.astype(BF).astype(F32)
    row = lax.broadcasted_iota(jnp.int32, (EXTRA, g.shape[1]), 0)
    extra = jnp.where(row == 0, high, jnp.where(row == 1, combine - high, 0.0))
    out_ref[2 * units :, :] = extra.astype(BF)


def input_kernel(capacity, all_ref, gate_ref, up_ref, out_ref, wide_ref, rows_ref):
    nodes, height, slots = all_ref.shape
    units = (height - EXTRA) // 2
    features = gate_ref.shape[0]
    gate_pre = all_ref[:, :units, :].reshape(nodes * units, slots)
    up_pre = all_ref[:, units : 2 * units, :].reshape(nodes * units, slots)
    wide_ref[:features, :slots] = dot(gate_ref[...], gate_pre, NN) + dot(up_ref[...], up_pre, NN)
    extra = all_ref[0, 2 * units :, :].astype(F32)
    for n in range(1, nodes):
        extra += all_ref[n, 2 * units :, :].astype(F32)
    spare = wide_ref.shape[0] - features
    wide_ref[features:, :slots] = jnp.broadcast_to(extra[0:1] + extra[1:2], (spare, slots))
    beyond = wide_ref.shape[1] - slots
    if beyond:
        wide_ref[:, slots:] = jnp.zeros((wide_ref.shape[0], beyond), F32)
    rows_ref[...] = wide_ref[...].T
    full, _, rows = layout(features, capacity)
    tight, wide = GROUP * capacity, GROUP * rows
    groups = slots // tight
    packs = packing(features, capacity, True)
    _, slot = slot_of_row((tight, LANES), 0, capacity)
    lane = lax.broadcasted_iota(jnp.int32, (tight, LANES), 1)
    for g in range(0, groups, 2):
        pieces = []
        for h in (g, g + 1):
            at = slice(h * tight, (h + 1) * tight)
            mine = [rows_ref[at, c * LANES : (c + 1) * LANES] for c in range(full + 1)]
            tail = mine.pop()
            turned = pltpu.roll(tail, 64, 1)
            mine.append(jnp.where((lane >= 64) == odd(slot), jnp.where(odd(slot), turned, tail), 0.0))
            scalar = jnp.where(lane < 64, turned, tail)
            mine.append(jnp.where(lane == slot, scalar, 0.0))
            pieces.append([piece.astype(BF) for piece in mine])
        total = jnp.zeros((wide, 2 * LANES), F32)
        for pack, low, high in zip(packs, *pieces):
            total += dot(pack, jnp.concatenate([low, high], axis=1), NN)
        for h in range(2):
            out_ref[(g + h) * wide : (g + h + 1) * wide, :] = total[
                :, h * LANES : (h + 1) * LANES
            ].astype(BF)


def collect_kernel(capacity, back_ref, rank_ref, ids_ref, grad_ref, combine_ref):
    experts, tokens = rank_ref.shape
    features = grad_ref.shape[0]
    full, scalars, rows = layout(features, capacity)
    rank = rank_ref[...]
    values = back_ref[...].astype(F32)
    turned = values.T.astype(BF)
    sums = [dot(turned, pick, NN) for pick in picks(rank, features, capacity)]
    for c in range(full):
        grad_ref[c * LANES : (c + 1) * LANES, :] = sums[c].astype(BF)
    grad_ref[full * LANES :, :] = (sums[full][:64] + sums[full + 1][64:]).astype(BF)
    height = -(-capacity // 8) * 8
    carried = values.reshape(experts, rows, LANES)[:, scalars : scalars + 1, :]
    column = jnp.sum(carried * slot_diagonal(height), axis=2, keepdims=True)
    j = lax.broadcasted_iota(jnp.int32, (experts, height, tokens), 1).astype(F32)
    chosen = jnp.sum(jnp.where(rank[:, None, :] == j, column, 0.0), axis=1)
    expert = lax.broadcasted_iota(jnp.int32, (experts, tokens), 0)
    for k in range(ids_ref.shape[0]):
        hit = ids_ref[k : k + 1, :] == expert
        combine_ref[k : k + 1, :] = jnp.sum(jnp.where(hit, chosen, 0.0), axis=0, keepdims=True)


def body(out_grad, gate_weights, expert_ids, w_gate, w_up, w_down, saved_gate, saved_up):
    experts = lax.axis_size("local")
    nodes = lax.axis_size("node")
    tokens, features = out_grad.shape
    top = expert_ids.shape[1]
    units, slots = saved_gate.shape[1:]
    hidden = w_down.shape[1]
    shape = jax.ShapeDtypeStruct
    swap = [(i, i ^ 1) for i in range(nodes)]

    capacity = slots // experts
    rows = layout(features, capacity)[2]
    lanes = -(-features // LANES) * LANES
    ids = expert_ids.T
    send, rank = call(
        functools.partial(dispatch_kernel, capacity),
        (shape((experts * rows, LANES), BF), shape((experts, tokens), F32)),
        ids,
        gate_weights.T,
        out_grad.T,
        plain=True,
    )
    arrived = lax.all_to_all(
        send.reshape(experts, rows, LANES), "local", split_axis=0, concat_axis=0, tiled=True
    )
    node = lax.axis_index("node")
    weights = call(
        weights_kernel,
        shape((2, hidden // 2, features), BF),
        jnp.stack([node % 2, node // 2]).astype(jnp.int32),
        w_down[0].T,
        smem=1,
        scratch=[pltpu.VMEM((2, hidden // LANES, 64, features), F32)],
    )
    rounded = -(-slots // LANES) * LANES
    other, packed, slot_gate = call(
        functools.partial(other_half_kernel, capacity),
        (shape((hidden // 2, rounded), BF), shape((slots, lanes), BF), shape((8, slots), F32)),
        arrived.reshape(experts * rows, LANES),
        weights,
    )
    depth = nodes // 2
    own, *others = call(
        own_half_kernel,
        [shape((units, rounded), BF if step else F32) for step in range(depth)],
        packed,
        weights,
        lax.ppermute(other, "node", swap),
    )
    parts = [own]
    for step in sorted(range(1, depth), key=lambda step: -min(step, depth - step)):
        onward = [(n, (n + 2 * step) % nodes) for n in range(nodes)]
        parts.append(lax.ppermute(others[step - 1], "node", onward))
    piece = call(
        hidden_kernel,
        shape((2 * units + EXTRA, slots), BF),
        saved_gate[0],
        saved_up[0],
        slot_gate,
        *parts,
    )
    gathered = lax.all_gather(piece, "node", axis=0, tiled=False)
    back = call(
        functools.partial(input_kernel, capacity),
        shape((experts * rows, LANES), BF),
        gathered,
        w_gate[0],
        w_up[0],
        scratch=[pltpu.VMEM((lanes, rounded), F32), pltpu.VMEM((rounded, lanes), F32)],
    )
    returned = lax.all_to_all(
        back.reshape(experts, rows, LANES), "local", split_axis=0, concat_axis=0, tiled=True
    )
    grad, combine = call(
        functools.partial(collect_kernel, capacity),
        (shape((features, tokens), BF), shape((top, tokens), F32)),
        returned.reshape(experts * rows, LANES),
        rank,
        ids,
    )
    return grad.T, combine.T.astype(BF)


def solution(mesh):
    in_specs = (
        P("local", "node"),
        P("local", None),
        P("local", None),
        P("local", "node", None),
        P("local", "node", None),
        P("local", None, "node"),
        P("local", "node", None),
        P("local", "node", None),
    )
    out_specs = (P("local", "node"), P("local", None))
    return jax.shard_map(body, mesh=mesh, in_specs=in_specs, out_specs=out_specs, check_vma=False)
```

```python
import functools

import jax
import jax.numpy as jnp
from jax import lax
from jax.experimental import pallas as pl
from jax.experimental.pallas import tpu as pltpu
from jax.sharding import PartitionSpec as P

BF = jnp.bfloat16
F32 = jnp.float32
LANES = 128
GROUP = 8
EXTRA = 16


def call(kernel, outs, *operands, smem=0, scratch=(), plain=False, mib=32):
    vmem = pl.BlockSpec() if plain else pl.BlockSpec(memory_space=pltpu.VMEM)
    spec = [pl.BlockSpec(memory_space=pltpu.SMEM)] * smem
    spec += [vmem] * (len(operands) - smem)
    return pl.pallas_call(
        kernel,
        out_shape=outs,
        in_specs=spec,
        out_specs=jax.tree.map(lambda _: vmem, outs),
        scratch_shapes=list(scratch),
        compiler_params=pltpu.CompilerParams(vmem_limit_bytes=mib * 2**20),
    )(*operands)


def dot(a, b, dims):
    return lax.dot_general(a, b, (dims, ((), ())), preferred_element_type=F32)


NN = ((1,), (0,))
NT = ((1,), (1,))


def layout(features, capacity):
    full = features // LANES
    scalars = full * capacity + (capacity + 1) // 2
    return full, scalars, -(-(scalars + 1) // 16) * 16


def place_codes(features, capacity):
    full, scalars, rows = layout(features, capacity)
    q = lax.broadcasted_iota(jnp.int32, (rows, LANES), 0)
    codes = []
    for c in range(full):
        at = q - c * capacity
        codes.append(jnp.where((at >= 0) & (at < capacity), at, -2))
    at = 2 * (q - full * capacity)
    tail = (at >= 0) & (q < scalars)
    codes.append(jnp.where(tail, at, -2))
    codes.append(jnp.where(tail & (at + 1 < capacity), at + 1, -2))
    return [code.astype(F32).astype(BF) for code in codes]


def picks(rank, features, capacity):
    experts, tokens = rank.shape
    one, zero = jnp.ones((), BF), jnp.zeros((), BF)
    place = rank.astype(BF)[:, None, :]
    out = []
    for code in place_codes(features, capacity):
        hit = jnp.where(place == code[None], one, zero)
        out.append(hit.reshape(experts * code.shape[0], tokens))
    return out


def slot_diagonal(height):
    j = lax.broadcasted_iota(jnp.int32, (1, height, LANES), 1)
    lane = lax.broadcasted_iota(jnp.int32, (1, height, LANES), 2)
    return jnp.where(j == lane, 1.0, 0.0).astype(F32)


def slot_of_row(shape, dim, capacity):
    r = lax.broadcasted_iota(jnp.int32, shape, dim)
    source = jnp.zeros(shape, jnp.int32)
    for s in range(1, GROUP):
        source += jnp.where(r >= s * capacity, 1, 0)
    return source, r - source * capacity


def packing(features, capacity, rows_first):
    full, scalars, rows = layout(features, capacity)
    tight, wide = GROUP * capacity, GROUP * rows
    shape = (wide, tight) if rows_first else (tight, wide)
    source, slot = slot_of_row(shape, 1 if rows_first else 0, capacity)
    at = lax.broadcasted_iota(jnp.int32, shape, 0 if rows_first else 1) - source * rows
    targets = [slot + c * capacity for c in range(full)]
    targets += [lax.shift_right_logical(slot, 1) + full * capacity, scalars]
    return [jnp.where(at == target, 1.0, 0.0).astype(BF) for target in targets]


def odd(slot):
    return (slot & 1) == 1


def dispatch_kernel(capacity, ids_ref, gates_ref, grad_ref, send_ref, rank_ref):
    experts, tokens = rank_ref.shape
    features = grad_ref.shape[0]
    full, scalars, rows = layout(features, capacity)
    expert = lax.broadcasted_iota(jnp.int32, (experts, tokens), 0)
    mask = jnp.zeros((experts, tokens), F32)
    weight = jnp.zeros((experts, tokens), F32)
    for k in range(ids_ref.shape[0]):
        hit = ids_ref[k : k + 1, :] == expert
        mask = jnp.where(hit, 1.0, mask)
        weight = jnp.where(hit, gates_ref[k : k + 1, :].astype(F32), weight)
    earlier = lax.broadcasted_iota(jnp.int32, (tokens, tokens), 0) < lax.broadcasted_iota(
        jnp.int32, (tokens, tokens), 1
    )
    rank = dot(mask.astype(BF), jnp.where(earlier, 1.0, 0.0).astype(BF), NN)
    rank = jnp.where(mask > 0.0, rank, -1.0)
    rank_ref[...] = rank
    height = -(-capacity // 8) * 8
    j = lax.broadcasted_iota(jnp.int32, (experts, height, tokens), 1).astype(F32)
    gate = jnp.where(rank[:, None, :] == j, weight[:, None, :], 0.0)
    gate = jnp.sum(gate, axis=2, keepdims=True)
    gate = jnp.sum(gate * slot_diagonal(height), axis=1, keepdims=True)
    tail = grad_ref[full * LANES :, :]
    empty = jnp.zeros((LANES - tail.shape[0], tokens), BF)
    pieces = [grad_ref[c * LANES : (c + 1) * LANES, :] for c in range(full)]
    pieces += [jnp.concatenate([tail, empty], axis=0), jnp.concatenate([empty, tail], axis=0)]
    total = jnp.zeros((experts * rows, LANES), F32)
    for pick, piece in zip(picks(rank, features, capacity), pieces):
        total += dot(pick, piece, NT)
    q = lax.broadcasted_iota(jnp.int32, (experts, rows, LANES), 1)
    total = jnp.where(q == scalars, gate, total.reshape(experts, rows, LANES))
    send_ref[...] = total.reshape(experts * rows, LANES).astype(BF)


def weights_kernel(place_ref, down_ref, out_ref, rows_ref):
    core, start = place_ref[0], place_ref[1]
    features, hidden = down_ref.shape
    blocks = hidden // LANES
    rows = down_ref[...].astype(F32).T.reshape(blocks, LANES, features)
    low, high = rows[:, :64], rows[:, 64:]
    rows_ref[0] = jnp.where(core == 0, low, high)
    rows_ref[1] = jnp.where(core == 0, high, low)
    for step in range(blocks):
        block = lax.rem(start + step, blocks)
        for half in range(2):
            out_ref[half, step * 64 : (step + 1) * 64, :] = rows_ref[half, block].astype(BF)


def other_half_kernel(capacity, arrived_ref, weight_ref, out_ref, rows_ref, gate_ref):
    features = weight_ref.shape[2]
    full, _, rows = layout(features, capacity)
    tight, wide = GROUP * capacity, GROUP * rows
    groups = arrived_ref.shape[0] // wide
    packs = packing(features, capacity, False)
    _, slot = slot_of_row((tight, LANES), 0, capacity)
    lane = lax.broadcasted_iota(jnp.int32, (tight, LANES), 1)
    for g in range(0, groups, 2):
        pair = jnp.concatenate(
            [arrived_ref[h * wide : (h + 1) * wide, :] for h in (g, g + 1)], axis=1
        )
        at = slice(g * tight, (g + 2) * tight)
        got = [dot(pack, pair, NN) for pack in packs]
        for c in range(full + 1):
            halves = []
            for h in range(2):
                piece = got[c][:, h * LANES : (h + 1) * LANES]
                if c == full:
                    gates = got[full + 1][:, h * LANES : (h + 1) * LANES]
                    gate = jnp.sum(jnp.where(lane == slot, gates, 0.0), axis=1, keepdims=True)
                    piece = jnp.where(odd(slot), pltpu.roll(piece, 64, 1), piece)
                    piece = jnp.where(lane < 64, piece, gate)
                halves.append(piece)
            rows_ref[at, c * LANES : (c + 1) * LANES] = jnp.concatenate(halves, axis=0).astype(BF)
    slots = rows_ref.shape[0]
    out_ref[:, :slots] = dot(weight_ref[1], rows_ref[:, :features], NT).astype(BF)
    if out_ref.shape[1] > slots:
        out_ref[:, slots:] = jnp.zeros((out_ref.shape[0], out_ref.shape[1] - slots), BF)
    lane = lax.broadcasted_iota(jnp.int32, (8, LANES), 1)
    at = jnp.where(lane == 64, 1.0, 0.0).astype(BF)
    gate_ref[...] = dot(at, rows_ref[:, full * LANES :], NT)


def own_half_kernel(rows_ref, weight_ref, partner_ref, *out_refs):
    features = weight_ref.shape[2]
    slots = rows_ref.shape[0]
    units = out_refs[0].shape[0]
    total = dot(weight_ref[0], rows_ref[:, :features], NT) + partner_ref[:, :slots].astype(F32)
    for step, out_ref in enumerate(out_refs):
        out_ref[:, :slots] = total[step * units : (step + 1) * units].astype(out_ref.dtype)
        if out_ref.shape[1] > slots:
            out_ref[:, slots:] = jnp.zeros((units, out_ref.shape[1] - slots), out_ref.dtype)


def hidden_kernel(gate_ref, up_ref, slot_gate_ref, *refs):
    *parts, out_ref = refs
    slots = gate_ref.shape[1]
    raw = parts[0][:, :slots].astype(F32)
    for part in parts[1:]:
        raw += part[:, :slots].astype(F32)
    g = gate_ref[...].astype(F32)
    u = up_ref[...].astype(F32)
    sigma = 1.0 / (1.0 + jnp.exp(-g))
    activ = g * sigma
    slope = sigma * (1.0 + g * (1.0 - sigma))
    combine = jnp.sum(raw * activ * u, axis=0, keepdims=True)
    scaled = raw * slot_gate_ref[0:1, :]
    units = g.shape[0]
    out_ref[:units, :] = (scaled * u * slope).astype(BF)
    out_ref[units : 2 * units, :] = (scaled * activ).astype(BF)
    high = combine.astype(BF).astype(F32)
    row = lax.broadcasted_iota(jnp.int32, (EXTRA, g.shape[1]), 0)
    extra = jnp.where(row == 0, high, jnp.where(row == 1, combine - high, 0.0))
    out_ref[2 * units :, :] = extra.astype(BF)


def input_kernel(capacity, all_ref, gate_ref, up_ref, out_ref, wide_ref, rows_ref):
    part, height, slots = all_ref.shape
    units = (height - EXTRA) // 2
    features = gate_ref.shape[0]
    step = pl.program_id(0)

    @pl.when(step == 0)
    def _():
        wide_ref[...] = jnp.zeros(wide_ref.shape, F32)

    gate_pre = all_ref[:, :units, :].reshape(part * units, slots)
    up_pre = all_ref[:, units : 2 * units, :].reshape(part * units, slots)
    wide_ref[:features, :slots] += dot(gate_ref[...], gate_pre, NN) + dot(up_ref[...], up_pre, NN)
    extra = all_ref[0, 2 * units :, :].astype(F32)
    for n in range(1, part):
        extra += all_ref[n, 2 * units :, :].astype(F32)
    spare = wide_ref.shape[0] - features
    wide_ref[features:, :slots] += jnp.broadcast_to(extra[0:1] + extra[1:2], (spare, slots))

    @pl.when(step == pl.num_programs(0) - 1)
    def _():
        pack_rows(capacity, slots, features, out_ref, wide_ref, rows_ref)


def pack_rows(capacity, slots, features, out_ref, wide_ref, rows_ref):
    rows_ref[...] = wide_ref[...].T
    full, _, rows = layout(features, capacity)
    tight, wide = GROUP * capacity, GROUP * rows
    groups = slots // tight
    packs = packing(features, capacity, True)
    _, slot = slot_of_row((tight, LANES), 0, capacity)
    lane = lax.broadcasted_iota(jnp.int32, (tight, LANES), 1)
    for g in range(0, groups, 2):
        pieces = []
        for h in (g, g + 1):
            at = slice(h * tight, (h + 1) * tight)
            mine = [rows_ref[at, c * LANES : (c + 1) * LANES] for c in range(full + 1)]
            tail = mine.pop()
            turned = pltpu.roll(tail, 64, 1)
            mine.append(jnp.where((lane >= 64) == odd(slot), jnp.where(odd(slot), turned, tail), 0.0))
            scalar = jnp.where(lane < 64, turned, tail)
            mine.append(jnp.where(lane == slot, scalar, 0.0))
            pieces.append([piece.astype(BF) for piece in mine])
        total = jnp.zeros((wide, 2 * LANES), F32)
        for pack, low, high in zip(packs, *pieces):
            total += dot(pack, jnp.concatenate([low, high], axis=1), NN)
        for h in range(2):
            out_ref[(g + h) * wide : (g + h + 1) * wide, :] = total[
                :, h * LANES : (h + 1) * LANES
            ].astype(BF)


def collect_kernel(capacity, back_ref, rank_ref, ids_ref, grad_ref, combine_ref):
    experts, tokens = rank_ref.shape
    features = grad_ref.shape[0]
    full, scalars, rows = layout(features, capacity)
    rank = rank_ref[...]
    values = back_ref[...].astype(F32)
    turned = values.T.astype(BF)
    sums = [dot(turned, pick, NN) for pick in picks(rank, features, capacity)]
    for c in range(full):
        grad_ref[c * LANES : (c + 1) * LANES, :] = sums[c].astype(BF)
    grad_ref[full * LANES :, :] = (sums[full][:64] + sums[full + 1][64:]).astype(BF)
    height = -(-capacity // 8) * 8
    carried = values.reshape(experts, rows, LANES)[:, scalars : scalars + 1, :]
    column = jnp.sum(carried * slot_diagonal(height), axis=2, keepdims=True)
    j = lax.broadcasted_iota(jnp.int32, (experts, height, tokens), 1).astype(F32)
    chosen = jnp.sum(jnp.where(rank[:, None, :] == j, column, 0.0), axis=1)
    expert = lax.broadcasted_iota(jnp.int32, (experts, tokens), 0)
    combine = []
    for k in range(ids_ref.shape[0]):
        hit = ids_ref[k : k + 1, :] == expert
        combine.append(jnp.sum(jnp.where(hit, chosen, 0.0), axis=0, keepdims=True))
    combine_ref[...] = jnp.concatenate(combine, axis=0).astype(BF)


def body(out_grad, gate_weights, expert_ids, w_gate, w_up, w_down, saved_gate, saved_up):
    experts = lax.axis_size("local")
    nodes = lax.axis_size("node")
    tokens, features = out_grad.shape
    top = expert_ids.shape[1]
    units, slots = saved_gate.shape[1:]
    hidden = w_down.shape[1]
    shape = jax.ShapeDtypeStruct
    swap = [(i, i ^ 1) for i in range(nodes)]

    capacity = slots // experts
    rows = layout(features, capacity)[2]
    lanes = -(-features // LANES) * LANES
    ids = expert_ids.T
    send, rank = call(
        functools.partial(dispatch_kernel, capacity),
        (shape((experts * rows, LANES), BF), shape((experts, tokens), F32)),
        ids,
        gate_weights.T,
        out_grad.T,
        plain=True,
        mib=60,
    )
    arrived = lax.all_to_all(
        send.reshape(experts, rows, LANES), "local", split_axis=0, concat_axis=0, tiled=True
    )
    node = lax.axis_index("node")
    weights = call(
        weights_kernel,
        shape((2, hidden // 2, features), BF),
        jnp.stack([node % 2, node // 2]).astype(jnp.int32),
        w_down[0].T,
        smem=1,
        scratch=[pltpu.VMEM((2, hidden // LANES, 64, features), F32)],
    )
    rounded = -(-slots // LANES) * LANES
    other, packed, slot_gate = call(
        functools.partial(other_half_kernel, capacity),
        (shape((hidden // 2, rounded), BF), shape((slots, lanes), BF), shape((8, slots), F32)),
        arrived.reshape(experts * rows, LANES),
        weights,
    )
    depth = nodes // 2
    own, *others = call(
        own_half_kernel,
        [shape((units, rounded), BF if step else F32) for step in range(depth)],
        packed,
        weights,
        lax.ppermute(other, "node", swap),
    )
    parts = [own]
    for step in sorted(range(1, depth), key=lambda step: -min(step, depth - step)):
        onward = [(n, (n + 2 * step) % nodes) for n in range(nodes)]
        parts.append(lax.ppermute(others[step - 1], "node", onward))
    piece = call(
        hidden_kernel,
        shape((2 * units + EXTRA, slots), BF),
        saved_gate[0],
        saved_up[0],
        slot_gate,
        *parts,
    )
    gathered = lax.all_gather(piece, "node", axis=0, tiled=False)
    part = 4 if nodes >= 8 else 2
    weight_spec = pl.BlockSpec((features, part * units), lambda n: (0, n))
    back = pl.pallas_call(
        functools.partial(input_kernel, capacity),
        out_shape=shape((experts * rows, LANES), BF),
        grid=(nodes // part,),
        in_specs=[
            pl.BlockSpec((part, 2 * units + EXTRA, slots), lambda n: (n, 0, 0)),
            weight_spec,
            weight_spec,
        ],
        out_specs=pl.BlockSpec((experts * rows, LANES), lambda n: (0, 0)),
        scratch_shapes=[pltpu.VMEM((lanes, rounded), F32), pltpu.VMEM((rounded, lanes), F32)],
        compiler_params=pltpu.CompilerParams(vmem_limit_bytes=60 * 2**20),
    )(gathered, w_gate[0], w_up[0])
    returned = lax.all_to_all(
        back.reshape(experts, rows, LANES), "local", split_axis=0, concat_axis=0, tiled=True
    )
    grad, combine = call(
        functools.partial(collect_kernel, capacity),
        (shape((features, tokens), BF), shape((top, tokens), BF)),
        returned.reshape(experts * rows, LANES),
        rank,
        ids,
    )
    return grad.T, combine.T


def solution(mesh):
    in_specs = (
        P("local", "node"),
        P("local", None),
        P("local", None),
        P("local", "node", None),
        P("local", "node", None),
        P("local", None, "node"),
        P("local", "node", None),
        P("local", "node", None),
    )
    out_specs = (P("local", "node"), P("local", None))
    return jax.shard_map(body, mesh=mesh, in_specs=in_specs, out_specs=out_specs, check_vma=False)
```

```python
import functools

import jax
import jax.numpy as jnp
from jax import lax
from jax.experimental import pallas as pl
from jax.experimental.pallas import tpu as pltpu
from jax.sharding import PartitionSpec as P

BF = jnp.bfloat16
F32 = jnp.float32
LANES = 128
GROUP = 8
EXTRA = 16


def call(kernel, outs, *operands, smem=0, scratch=(), plain=False, mib=32):
    vmem = pl.BlockSpec() if plain else pl.BlockSpec(memory_space=pltpu.VMEM)
    spec = [pl.BlockSpec(memory_space=pltpu.SMEM)] * smem
    spec += [vmem] * (len(operands) - smem)
    return pl.pallas_call(
        kernel,
        out_shape=outs,
        in_specs=spec,
        out_specs=jax.tree.map(lambda _: vmem, outs),
        scratch_shapes=list(scratch),
        compiler_params=pltpu.CompilerParams(vmem_limit_bytes=mib * 2**20),
    )(*operands)


def dot(a, b, dims):
    return lax.dot_general(a, b, (dims, ((), ())), preferred_element_type=F32)


NN = ((1,), (0,))
NT = ((1,), (1,))


def layout(features, capacity):
    full = features // LANES
    scalars = full * capacity + (capacity + 1) // 2
    return full, scalars, -(-(scalars + 1) // 16) * 16


def place_codes(features, capacity):
    full, scalars, rows = layout(features, capacity)
    q = lax.broadcasted_iota(jnp.int32, (rows, LANES), 0)
    codes = []
    for c in range(full):
        at = q - c * capacity
        codes.append(jnp.where((at >= 0) & (at < capacity), at, -2))
    at = 2 * (q - full * capacity)
    tail = (at >= 0) & (q < scalars)
    codes.append(jnp.where(tail, at, -2))
    codes.append(jnp.where(tail & (at + 1 < capacity), at + 1, -2))
    return [code.astype(F32).astype(BF) for code in codes]


def picks(rank, features, capacity):
    experts, tokens = rank.shape
    one, zero = jnp.ones((), BF), jnp.zeros((), BF)
    place = rank.astype(BF)[:, None, :]
    out = []
    for code in place_codes(features, capacity):
        hit = jnp.where(place == code[None], one, zero)
        out.append(hit.reshape(experts * code.shape[0], tokens))
    return out


def slot_diagonal(height):
    j = lax.broadcasted_iota(jnp.int32, (1, height, LANES), 1)
    lane = lax.broadcasted_iota(jnp.int32, (1, height, LANES), 2)
    return jnp.where(j == lane, 1.0, 0.0).astype(F32)


def slot_of_row(shape, dim, capacity):
    r = lax.broadcasted_iota(jnp.int32, shape, dim)
    source = jnp.zeros(shape, jnp.int32)
    for s in range(1, GROUP):
        source += jnp.where(r >= s * capacity, 1, 0)
    return source, r - source * capacity


def packing(features, capacity, rows_first):
    full, scalars, rows = layout(features, capacity)
    tight, wide = GROUP * capacity, GROUP * rows
    shape = (wide, tight) if rows_first else (tight, wide)
    source, slot = slot_of_row(shape, 1 if rows_first else 0, capacity)
    at = lax.broadcasted_iota(jnp.int32, shape, 0 if rows_first else 1) - source * rows
    targets = [slot + c * capacity for c in range(full)]
    targets += [lax.shift_right_logical(slot, 1) + full * capacity, scalars]
    return [jnp.where(at == target, 1.0, 0.0).astype(BF) for target in targets]


def odd(slot):
    return (slot & 1) == 1


def dispatch_kernel(capacity, ids_ref, gates_ref, grad_ref, send_ref, rank_ref):
    experts, tokens = rank_ref.shape
    features = grad_ref.shape[0]
    full, scalars, rows = layout(features, capacity)
    expert = lax.broadcasted_iota(jnp.int32, (experts, tokens), 0)
    mask = jnp.zeros((experts, tokens), F32)
    weight = jnp.zeros((experts, tokens), F32)
    for k in range(ids_ref.shape[0]):
        hit = ids_ref[k : k + 1, :] == expert
        mask = jnp.where(hit, 1.0, mask)
        weight = jnp.where(hit, gates_ref[k : k + 1, :].astype(F32), weight)
    earlier = lax.broadcasted_iota(jnp.int32, (tokens, tokens), 0) < lax.broadcasted_iota(
        jnp.int32, (tokens, tokens), 1
    )
    rank = dot(mask.astype(BF), jnp.where(earlier, 1.0, 0.0).astype(BF), NN)
    rank = jnp.where(mask > 0.0, rank, -1.0)
    rank_ref[...] = rank
    height = -(-capacity // 8) * 8
    j = lax.broadcasted_iota(jnp.int32, (experts, height, tokens), 1).astype(F32)
    gate = jnp.where(rank[:, None, :] == j, weight[:, None, :], 0.0)
    gate = jnp.sum(gate, axis=2, keepdims=True)
    gate = jnp.sum(gate * slot_diagonal(height), axis=1, keepdims=True)
    tail = grad_ref[full * LANES :, :]
    empty = jnp.zeros((LANES - tail.shape[0], tokens), BF)
    pieces = [grad_ref[c * LANES : (c + 1) * LANES, :] for c in range(full)]
    pieces += [jnp.concatenate([tail, empty], axis=0), jnp.concatenate([empty, tail], axis=0)]
    total = jnp.zeros((experts * rows, LANES), F32)
    for pick, piece in zip(picks(rank, features, capacity), pieces):
        total += dot(pick, piece, NT)
    q = lax.broadcasted_iota(jnp.int32, (experts, rows, LANES), 1)
    total = jnp.where(q == scalars, gate, total.reshape(experts, rows, LANES))
    send_ref[...] = total.reshape(experts * rows, LANES).astype(BF)


def weights_kernel(place_ref, down_ref, out_ref, rows_ref):
    core, start = place_ref[0], place_ref[1]
    features, hidden = down_ref.shape
    blocks = hidden // LANES
    rows = down_ref[...].astype(F32).T.reshape(blocks, LANES, features)
    low, high = rows[:, :64], rows[:, 64:]
    rows_ref[0] = jnp.where(core == 0, low, high)
    rows_ref[1] = jnp.where(core == 0, high, low)
    kept = blocks // 2
    for half in range(2):
        for i in range(kept):
            block = lax.rem(start + 2 * i, blocks)
            out_ref[half, i * 64 : (i + 1) * 64, :] = rows_ref[half, block].astype(BF)
        for side in range(2):
            at = kept * (64 + side * 32)
            for i in range(kept):
                block = lax.rem(place_ref[2 + side] + 2 * i, blocks)
                part = rows_ref[half, block, side * 32 : (side + 1) * 32, :]
                out_ref[half, at + i * 32 : at + (i + 1) * 32, :] = part.astype(BF)


def other_half_kernel(capacity, arrived_ref, weight_ref, out_ref, rows_ref, gate_ref):
    features = weight_ref.shape[2]
    full, _, rows = layout(features, capacity)
    tight, wide = GROUP * capacity, GROUP * rows
    groups = arrived_ref.shape[0] // wide
    packs = packing(features, capacity, False)
    _, slot = slot_of_row((tight, LANES), 0, capacity)
    lane = lax.broadcasted_iota(jnp.int32, (tight, LANES), 1)
    for g in range(0, groups, 2):
        pair = jnp.concatenate(
            [arrived_ref[h * wide : (h + 1) * wide, :] for h in (g, g + 1)], axis=1
        )
        at = slice(g * tight, (g + 2) * tight)
        got = [dot(pack, pair, NN) for pack in packs]
        for c in range(full + 1):
            halves = []
            for h in range(2):
                piece = got[c][:, h * LANES : (h + 1) * LANES]
                if c == full:
                    gates = got[full + 1][:, h * LANES : (h + 1) * LANES]
                    gate = jnp.sum(jnp.where(lane == slot, gates, 0.0), axis=1, keepdims=True)
                    piece = jnp.where(odd(slot), pltpu.roll(piece, 64, 1), piece)
                    piece = jnp.where(lane < 64, piece, gate)
                halves.append(piece)
            rows_ref[at, c * LANES : (c + 1) * LANES] = jnp.concatenate(halves, axis=0).astype(BF)
    slots = rows_ref.shape[0]
    out_ref[:, :slots] = dot(weight_ref[1], rows_ref[:, :features], NT).astype(BF)
    if out_ref.shape[1] > slots:
        out_ref[:, slots:] = jnp.zeros((out_ref.shape[0], out_ref.shape[1] - slots), BF)
    lane = lax.broadcasted_iota(jnp.int32, (8, LANES), 1)
    at = jnp.where(lane == 64, 1.0, 0.0).astype(BF)
    gate_ref[...] = dot(at, rows_ref[:, full * LANES :], NT)


def store_wide(out_ref, at, value):
    slots = value.shape[1]
    out_ref[at, :slots] = value.astype(out_ref.dtype)
    if out_ref.shape[1] > slots:
        rest = (value.shape[0], out_ref.shape[1] - slots)
        out_ref[at, slots:] = jnp.zeros(rest, out_ref.dtype)


def swapped_rows_kernel(rows_ref, weight_ref, partner_ref, *out_refs):
    features = weight_ref.shape[2]
    slots = rows_ref.shape[0]
    kept = weight_ref.shape[1] // 2
    total = dot(weight_ref[0, kept:, :], rows_ref[:, :features], NT)
    total += partner_ref[kept:, :slots].astype(F32)
    for side, out_ref in enumerate(out_refs):
        store_wide(out_ref, slice(None), total[side * kept // 2 : (side + 1) * kept // 2])


def kept_rows_kernel(rows_ref, weight_ref, partner_ref, low_ref, high_ref, *out_refs):
    features = weight_ref.shape[2]
    slots = rows_ref.shape[0]
    kept = weight_ref.shape[1] // 2
    total = dot(weight_ref[0, :kept, :], rows_ref[:, :features], NT)
    total += partner_ref[:kept, :slots].astype(F32)
    for i, out_ref in enumerate(out_refs):
        for side, swapped_ref in enumerate((low_ref, high_ref)):
            at = slice(i * 64 + side * 32, i * 64 + (side + 1) * 32)
            value = total[at] + swapped_ref[i * 32 : (i + 1) * 32, :slots].astype(F32)
            store_wide(out_ref, slice(side * 32, (side + 1) * 32), value)


def hidden_kernel(gate_ref, up_ref, slot_gate_ref, *refs):
    *parts, out_ref = refs
    slots = gate_ref.shape[1]
    raw = parts[0][:, :slots].astype(F32)
    for part in parts[1:]:
        raw += part[:, :slots].astype(F32)
    g = gate_ref[...].astype(F32)
    u = up_ref[...].astype(F32)
    sigma = 1.0 / (1.0 + jnp.exp(-g))
    activ = g * sigma
    slope = sigma * (1.0 + g * (1.0 - sigma))
    combine = jnp.sum(raw * activ * u, axis=0, keepdims=True)
    scaled = raw * slot_gate_ref[0:1, :]
    units = g.shape[0]
    out_ref[:units, :] = (scaled * u * slope).astype(BF)
    out_ref[units : 2 * units, :] = (scaled * activ).astype(BF)
    high = combine.astype(BF).astype(F32)
    row = lax.broadcasted_iota(jnp.int32, (EXTRA, g.shape[1]), 0)
    extra = jnp.where(row == 0, high, jnp.where(row == 1, combine - high, 0.0))
    out_ref[2 * units :, :] = extra.astype(BF)


def input_kernel(capacity, all_ref, gate_ref, up_ref, out_ref, wide_ref, rows_ref):
    nodes, height, slots = all_ref.shape
    units = (height - EXTRA) // 2
    features = gate_ref.shape[0]
    gate_pre = all_ref[:, :units, :].reshape(nodes * units, slots)
    up_pre = all_ref[:, units : 2 * units, :].reshape(nodes * units, slots)
    wide_ref[:features, :slots] = dot(gate_ref[...], gate_pre, NN) + dot(up_ref[...], up_pre, NN)
    extra = all_ref[0, 2 * units :, :].astype(F32)
    for n in range(1, nodes):
        extra += all_ref[n, 2 * units :, :].astype(F32)
    spare = wide_ref.shape[0] - features
    wide_ref[features:, :slots] = jnp.broadcast_to(extra[0:1] + extra[1:2], (spare, slots))
    beyond = wide_ref.shape[1] - slots
    if beyond:
        wide_ref[:, slots:] = jnp.zeros((wide_ref.shape[0], beyond), F32)
    rows_ref[...] = wide_ref[...].T
    full, _, rows = layout(features, capacity)
    tight, wide = GROUP * capacity, GROUP * rows
    groups = slots // tight
    packs = packing(features, capacity, True)
    _, slot = slot_of_row((tight, LANES), 0, capacity)
    lane = lax.broadcasted_iota(jnp.int32, (tight, LANES), 1)
    for g in range(0, groups, 2):
        pieces = []
        for h in (g, g + 1):
            at = slice(h * tight, (h + 1) * tight)
            mine = [rows_ref[at, c * LANES : (c + 1) * LANES] for c in range(full + 1)]
            tail = mine.pop()
            turned = pltpu.roll(tail, 64, 1)
            mine.append(jnp.where((lane >= 64) == odd(slot), jnp.where(odd(slot), turned, tail), 0.0))
            scalar = jnp.where(lane < 64, turned, tail)
            mine.append(jnp.where(lane == slot, scalar, 0.0))
            pieces.append([piece.astype(BF) for piece in mine])
        total = jnp.zeros((wide, 2 * LANES), F32)
        for pack, low, high in zip(packs, *pieces):
            total += dot(pack, jnp.concatenate([low, high], axis=1), NN)
        for h in range(2):
            out_ref[(g + h) * wide : (g + h + 1) * wide, :] = total[
                :, h * LANES : (h + 1) * LANES
            ].astype(BF)


def collect_kernel(capacity, back_ref, rank_ref, ids_ref, grad_ref, combine_ref):
    experts, tokens = rank_ref.shape
    features = grad_ref.shape[0]
    full, scalars, rows = layout(features, capacity)
    rank = rank_ref[...]
    values = back_ref[...].astype(F32)
    turned = values.T.astype(BF)
    sums = [dot(turned, pick, NN) for pick in picks(rank, features, capacity)]
    for c in range(full):
        grad_ref[c * LANES : (c + 1) * LANES, :] = sums[c].astype(BF)
    grad_ref[full * LANES :, :] = (sums[full][:64] + sums[full + 1][64:]).astype(BF)
    height = -(-capacity // 8) * 8
    carried = values.reshape(experts, rows, LANES)[:, scalars : scalars + 1, :]
    column = jnp.sum(carried * slot_diagonal(height), axis=2, keepdims=True)
    j = lax.broadcasted_iota(jnp.int32, (experts, height, tokens), 1).astype(F32)
    chosen = jnp.sum(jnp.where(rank[:, None, :] == j, column, 0.0), axis=1)
    expert = lax.broadcasted_iota(jnp.int32, (experts, tokens), 0)
    combine = []
    for k in range(ids_ref.shape[0]):
        hit = ids_ref[k : k + 1, :] == expert
        combine.append(jnp.sum(jnp.where(hit, chosen, 0.0), axis=0, keepdims=True))
    combine_ref[...] = jnp.concatenate(combine, axis=0).astype(BF)


def body(out_grad, gate_weights, expert_ids, w_gate, w_up, w_down, saved_gate, saved_up):
    experts = lax.axis_size("local")
    nodes = lax.axis_size("node")
    tokens, features = out_grad.shape
    top = expert_ids.shape[1]
    units, slots = saved_gate.shape[1:]
    hidden = w_down.shape[1]
    shape = jax.ShapeDtypeStruct
    swap = [(i, i ^ 1) for i in range(nodes)]

    capacity = slots // experts
    rows = layout(features, capacity)[2]
    lanes = -(-features // LANES) * LANES
    ids = expert_ids.T
    send, rank = call(
        functools.partial(dispatch_kernel, capacity),
        (shape((experts * rows, LANES), BF), shape((experts, tokens), F32)),
        ids,
        gate_weights.T,
        out_grad.T,
        plain=True,
        mib=60,
    )
    arrived = lax.all_to_all(
        send.reshape(experts, rows, LANES), "local", split_axis=0, concat_axis=0, tiled=True
    )
    node = lax.axis_index("node")
    depth = nodes // 2
    z = node // 2
    toward = 1 - 2 * (z % 2)
    weights = call(
        weights_kernel,
        shape((2, hidden // 2, features), BF),
        jnp.stack([node % 2, z, (z + toward) % depth, (z - toward) % depth]).astype(jnp.int32),
        w_down[0].T,
        smem=1,
        scratch=[pltpu.VMEM((2, hidden // LANES, 64, features), F32)],
    )
    rounded = -(-slots // LANES) * LANES
    other, packed, slot_gate = call(
        functools.partial(other_half_kernel, capacity),
        (shape((hidden // 2, rounded), BF), shape((slots, lanes), BF), shape((8, slots), F32)),
        arrived.reshape(experts * rows, LANES),
        weights,
    )
    partner = lax.ppermute(other, "node", swap)
    sides = call(
        swapped_rows_kernel,
        [shape((hidden // 8, rounded), BF)] * 2,
        packed,
        weights,
        partner,
    )
    pairs = [
        [(n, (n + 2 * sign * (1 - 2 * (n // 2 % 2))) % nodes) for n in range(nodes)]
        for sign in (1, -1)
    ]
    low, high = (lax.ppermute(side, "node", pair) for side, pair in zip(sides, pairs))
    own, *others = call(
        kept_rows_kernel,
        [shape((units, rounded), BF if step else F32) for step in range(depth // 2)],
        packed,
        weights,
        partner,
        low,
        high,
    )
    parts = [own]
    for step in sorted(range(1, depth // 2), key=lambda step: abs(step - depth // 4)):
        onward = [(n, (n + 4 * step) % nodes) for n in range(nodes)]
        parts.append(lax.ppermute(others[step - 1], "node", onward))
    piece = call(
        hidden_kernel,
        shape((2 * units + EXTRA, slots), BF),
        saved_gate[0],
        saved_up[0],
        slot_gate,
        *parts,
    )
    gathered = lax.all_gather(piece, "node", axis=0, tiled=False)
    back = call(
        functools.partial(input_kernel, capacity),
        shape((experts * rows, LANES), BF),
        gathered,
        w_gate[0],
        w_up[0],
        scratch=[pltpu.VMEM((lanes, rounded), F32), pltpu.VMEM((rounded, lanes), F32)],
    )
    returned = lax.all_to_all(
        back.reshape(experts, rows, LANES), "local", split_axis=0, concat_axis=0, tiled=True
    )
    grad, combine = call(
        functools.partial(collect_kernel, capacity),
        (shape((features, tokens), BF), shape((top, tokens), BF)),
        returned.reshape(experts * rows, LANES),
        rank,
        ids,
    )
    return grad.T, combine.T


def solution(mesh):
    in_specs = (
        P("local", "node"),
        P("local", None),
        P("local", None),
        P("local", "node", None),
        P("local", "node", None),
        P("local", None, "node"),
        P("local", "node", None),
        P("local", "node", None),
    )
    out_specs = (P("local", "node"), P("local", None))
    return jax.shard_map(body, mesh=mesh, in_specs=in_specs, out_specs=out_specs, check_vma=False)
```

```python
import functools

import jax
import jax.numpy as jnp
from jax import lax
from jax.experimental import pallas as pl
from jax.experimental.pallas import tpu as pltpu
from jax.sharding import PartitionSpec as P

BF = jnp.bfloat16
F32 = jnp.float32
LANES = 128
GROUP = 8
EXTRA = 16


def call(kernel, outs, *operands, smem=0, scratch=(), plain=False, mib=32):
    vmem = pl.BlockSpec() if plain else pl.BlockSpec(memory_space=pltpu.VMEM)
    spec = [pl.BlockSpec(memory_space=pltpu.SMEM)] * smem
    spec += [vmem] * (len(operands) - smem)
    return pl.pallas_call(
        kernel,
        out_shape=outs,
        in_specs=spec,
        out_specs=jax.tree.map(lambda _: vmem, outs),
        scratch_shapes=list(scratch),
        compiler_params=pltpu.CompilerParams(vmem_limit_bytes=mib * 2**20),
    )(*operands)


def dot(a, b, dims):
    return lax.dot_general(a, b, (dims, ((), ())), preferred_element_type=F32)


NN = ((1,), (0,))
NT = ((1,), (1,))


def layout(features, capacity):
    full = features // LANES
    scalars = full * capacity + (capacity + 1) // 2
    return full, scalars, -(-(scalars + 1) // 16) * 16


def place_codes(features, capacity):
    full, scalars, rows = layout(features, capacity)
    q = lax.broadcasted_iota(jnp.int32, (rows, LANES), 0)
    codes = []
    for c in range(full):
        at = q - c * capacity
        codes.append(jnp.where((at >= 0) & (at < capacity), at, -2))
    at = 2 * (q - full * capacity)
    tail = (at >= 0) & (q < scalars)
    codes.append(jnp.where(tail, at, -2))
    codes.append(jnp.where(tail & (at + 1 < capacity), at + 1, -2))
    return [code.astype(F32).astype(BF) for code in codes]


def picks(rank, features, capacity):
    experts, tokens = rank.shape
    one, zero = jnp.ones((), BF), jnp.zeros((), BF)
    place = rank.astype(BF)[:, None, :]
    out = []
    for code in place_codes(features, capacity):
        hit = jnp.where(place == code[None], one, zero)
        out.append(hit.reshape(experts * code.shape[0], tokens))
    return out


def slot_diagonal(height):
    j = lax.broadcasted_iota(jnp.int32, (1, height, LANES), 1)
    lane = lax.broadcasted_iota(jnp.int32, (1, height, LANES), 2)
    return jnp.where(j == lane, 1.0, 0.0).astype(F32)


def slot_of_row(shape, dim, capacity):
    r = lax.broadcasted_iota(jnp.int32, shape, dim)
    source = jnp.zeros(shape, jnp.int32)
    for s in range(1, GROUP):
        source += jnp.where(r >= s * capacity, 1, 0)
    return source, r - source * capacity


def packing(features, capacity, rows_first):
    full, scalars, rows = layout(features, capacity)
    tight, wide = GROUP * capacity, GROUP * rows
    shape = (wide, tight) if rows_first else (tight, wide)
    source, slot = slot_of_row(shape, 1 if rows_first else 0, capacity)
    at = lax.broadcasted_iota(jnp.int32, shape, 0 if rows_first else 1) - source * rows
    targets = [slot + c * capacity for c in range(full)]
    targets += [lax.shift_right_logical(slot, 1) + full * capacity, scalars]
    return [jnp.where(at == target, 1.0, 0.0).astype(BF) for target in targets]


def odd(slot):
    return (slot & 1) == 1


def dispatch_kernel(capacity, ids_ref, gates_ref, grad_ref, send_ref, rank_ref):
    experts, tokens = rank_ref.shape
    features = grad_ref.shape[0]
    full, scalars, rows = layout(features, capacity)
    expert = lax.broadcasted_iota(jnp.int32, (experts, tokens), 0)
    mask = jnp.zeros((experts, tokens), F32)
    weight = jnp.zeros((experts, tokens), F32)
    for k in range(ids_ref.shape[0]):
        hit = ids_ref[k : k + 1, :] == expert
        mask = jnp.where(hit, 1.0, mask)
        weight = jnp.where(hit, gates_ref[k : k + 1, :].astype(F32), weight)
    earlier = lax.broadcasted_iota(jnp.int32, (tokens, tokens), 0) < lax.broadcasted_iota(
        jnp.int32, (tokens, tokens), 1
    )
    rank = dot(mask.astype(BF), jnp.where(earlier, 1.0, 0.0).astype(BF), NN)
    rank = jnp.where(mask > 0.0, rank, -1.0)
    rank_ref[...] = rank
    height = -(-capacity // 8) * 8
    j = lax.broadcasted_iota(jnp.int32, (experts, height, tokens), 1).astype(F32)
    gate = jnp.where(rank[:, None, :] == j, weight[:, None, :], 0.0)
    gate = jnp.sum(gate, axis=2, keepdims=True)
    gate = jnp.sum(gate * slot_diagonal(height), axis=1, keepdims=True)
    tail = grad_ref[full * LANES :, :]
    empty = jnp.zeros((LANES - tail.shape[0], tokens), BF)
    pieces = [grad_ref[c * LANES : (c + 1) * LANES, :] for c in range(full)]
    pieces += [jnp.concatenate([tail, empty], axis=0), jnp.concatenate([empty, tail], axis=0)]
    total = dot(
        jnp.concatenate(picks(rank, features, capacity), axis=1),
        jnp.concatenate(pieces, axis=1),
        NT,
    )
    q = lax.broadcasted_iota(jnp.int32, (experts, rows, LANES), 1)
    total = jnp.where(q == scalars, gate, total.reshape(experts, rows, LANES))
    send_ref[...] = total.reshape(experts * rows, LANES).astype(BF)


def weights_kernel(place_ref, down_ref, out_ref, rows_ref):
    core, start = place_ref[0], place_ref[1]
    features, hidden = down_ref.shape
    blocks = hidden // LANES
    rows = down_ref[...].astype(F32).T.reshape(blocks, LANES, features)
    low, high = rows[:, :64], rows[:, 64:]
    rows_ref[0] = jnp.where(core == 0, low, high)
    rows_ref[1] = jnp.where(core == 0, high, low)
    for step in range(blocks):
        block = lax.rem(start + step, blocks)
        for half in range(2):
            out_ref[half, step * 64 : (step + 1) * 64, :] = rows_ref[half, block].astype(BF)


def other_half_kernel(capacity, arrived_ref, weight_ref, out_ref, rows_ref, gate_ref):
    features = weight_ref.shape[2]
    full, _, rows = layout(features, capacity)
    tight, wide = GROUP * capacity, GROUP * rows
    groups = arrived_ref.shape[0] // wide
    packs = packing(features, capacity, False)
    _, slot = slot_of_row((tight, LANES), 0, capacity)
    lane = lax.broadcasted_iota(jnp.int32, (tight, LANES), 1)
    for g in range(0, groups, 2):
        pair = jnp.concatenate(
            [arrived_ref[h * wide : (h + 1) * wide, :] for h in (g, g + 1)], axis=1
        )
        at = slice(g * tight, (g + 2) * tight)
        got = [dot(pack, pair, NN) for pack in packs]
        for c in range(full + 1):
            halves = []
            for h in range(2):
                piece = got[c][:, h * LANES : (h + 1) * LANES]
                if c == full:
                    gates = got[full + 1][:, h * LANES : (h + 1) * LANES]
                    gate = jnp.sum(jnp.where(lane == slot, gates, 0.0), axis=1, keepdims=True)
                    piece = jnp.where(odd(slot), pltpu.roll(piece, 64, 1), piece)
                    piece = jnp.where(lane < 64, piece, gate)
                halves.append(piece)
            rows_ref[at, c * LANES : (c + 1) * LANES] = jnp.concatenate(halves, axis=0).astype(BF)
    slots = rows_ref.shape[0]
    out_ref[:, :slots] = dot(weight_ref[1], rows_ref[:, :features], NT).astype(BF)
    if out_ref.shape[1] > slots:
        out_ref[:, slots:] = jnp.zeros((out_ref.shape[0], out_ref.shape[1] - slots), BF)
    lane = lax.broadcasted_iota(jnp.int32, (8, LANES), 1)
    at = jnp.where(lane == 64, 1.0, 0.0).astype(BF)
    gate_ref[...] = dot(at, rows_ref[:, full * LANES :], NT)


def store_wide(out_ref, at, value):
    slots = value.shape[1]
    out_ref[at, :slots] = value.astype(out_ref.dtype)
    if out_ref.shape[1] > slots:
        rest = (value.shape[0], out_ref.shape[1] - slots)
        out_ref[at, slots:] = jnp.zeros(rest, out_ref.dtype)


def own_half_kernel(rows_ref, weight_ref, partner_ref, *out_refs):
    features = weight_ref.shape[2]
    slots = rows_ref.shape[0]
    depth = len(out_refs) - 1
    total = dot(weight_ref[0], rows_ref[:, :features], NT) + partner_ref[:, :slots].astype(F32)
    for step in range(depth):
        block = total[step * 64 : (step + 1) * 64]
        if step == depth // 2:
            store_wide(out_refs[step], slice(None), block[:32])
            store_wide(out_refs[depth], slice(None), block[32:])
        else:
            store_wide(out_refs[step], slice(None), block)


def relay_kernel(up_ref, down_ref, low_ref, high_ref, up_out_ref, down_out_ref):
    up_out_ref[:32, :] = (up_ref[:32, :] + low_ref[...].astype(F32)).astype(BF)
    up_out_ref[32:, :] = up_ref[32:, :].astype(BF)
    down_out_ref[:32, :] = down_ref[:32, :].astype(BF)
    down_out_ref[32:, :] = (down_ref[32:, :] + high_ref[...].astype(F32)).astype(BF)


def hidden_kernel(gate_ref, up_ref, slot_gate_ref, *refs):
    *parts, out_ref = refs
    slots = gate_ref.shape[1]
    raw = parts[0][:, :slots].astype(F32)
    for part in parts[1:]:
        raw += part[:, :slots].astype(F32)
    g = gate_ref[...].astype(F32)
    u = up_ref[...].astype(F32)
    sigma = 1.0 / (1.0 + jnp.exp(-g))
    activ = g * sigma
    slope = sigma * (1.0 + g * (1.0 - sigma))
    combine = jnp.sum(raw * activ * u, axis=0, keepdims=True)
    scaled = raw * slot_gate_ref[0:1, :]
    units = g.shape[0]
    out_ref[:units, :] = (scaled * u * slope).astype(BF)
    out_ref[units : 2 * units, :] = (scaled * activ).astype(BF)
    high = combine.astype(BF).astype(F32)
    row = lax.broadcasted_iota(jnp.int32, (EXTRA, g.shape[1]), 0)
    extra = jnp.where(row == 0, high, jnp.where(row == 1, combine - high, 0.0))
    out_ref[2 * units :, :] = extra.astype(BF)


def input_kernel(capacity, all_ref, gate_ref, up_ref, out_ref, wide_ref, rows_ref):
    nodes, height, slots = all_ref.shape
    units = (height - EXTRA) // 2
    features = gate_ref.shape[0]
    gate_pre = all_ref[:, :units, :].reshape(nodes * units, slots)
    up_pre = all_ref[:, units : 2 * units, :].reshape(nodes * units, slots)
    wide_ref[:features, :slots] = dot(gate_ref[...], gate_pre, NN) + dot(up_ref[...], up_pre, NN)
    extra = all_ref[0, 2 * units :, :].astype(F32)
    for n in range(1, nodes):
        extra += all_ref[n, 2 * units :, :].astype(F32)
    spare = wide_ref.shape[0] - features
    wide_ref[features:, :slots] = jnp.broadcast_to(extra[0:1] + extra[1:2], (spare, slots))
    beyond = wide_ref.shape[1] - slots
    if beyond:
        wide_ref[:, slots:] = jnp.zeros((wide_ref.shape[0], beyond), F32)
    rows_ref[...] = wide_ref[...].T
    full, _, rows = layout(features, capacity)
    tight, wide = GROUP * capacity, GROUP * rows
    groups = slots // tight
    packs = packing(features, capacity, True)
    _, slot = slot_of_row((tight, LANES), 0, capacity)
    lane = lax.broadcasted_iota(jnp.int32, (tight, LANES), 1)
    for g in range(0, groups, 2):
        pieces = []
        for h in (g, g + 1):
            at = slice(h * tight, (h + 1) * tight)
            mine = [rows_ref[at, c * LANES : (c + 1) * LANES] for c in range(full + 1)]
            tail = mine.pop()
            turned = pltpu.roll(tail, 64, 1)
            mine.append(jnp.where((lane >= 64) == odd(slot), jnp.where(odd(slot), turned, tail), 0.0))
            scalar = jnp.where(lane < 64, turned, tail)
            mine.append(jnp.where(lane == slot, scalar, 0.0))
            pieces.append([piece.astype(BF) for piece in mine])
        total = jnp.zeros((wide, 2 * LANES), F32)
        for pack, low, high in zip(packs, *pieces):
            total += dot(pack, jnp.concatenate([low, high], axis=1), NN)
        for h in range(2):
            out_ref[(g + h) * wide : (g + h + 1) * wide, :] = total[
                :, h * LANES : (h + 1) * LANES
            ].astype(BF)


def collect_kernel(capacity, back_ref, rank_ref, ids_ref, grad_ref, combine_ref):
    experts, tokens = rank_ref.shape
    features = grad_ref.shape[0]
    full, scalars, rows = layout(features, capacity)
    rank = rank_ref[...]
    values = back_ref[...].astype(F32)
    turned = values.T.astype(BF)
    sums = [dot(turned, pick, NN) for pick in picks(rank, features, capacity)]
    for c in range(full):
        grad_ref[c * LANES : (c + 1) * LANES, :] = sums[c].astype(BF)
    grad_ref[full * LANES :, :] = (sums[full][:64] + sums[full + 1][64:]).astype(BF)
    height = -(-capacity // 8) * 8
    carried = values.reshape(experts, rows, LANES)[:, scalars : scalars + 1, :]
    column = jnp.sum(carried * slot_diagonal(height), axis=2, keepdims=True)
    j = lax.broadcasted_iota(jnp.int32, (experts, height, tokens), 1).astype(F32)
    chosen = jnp.sum(jnp.where(rank[:, None, :] == j, column, 0.0), axis=1)
    expert = lax.broadcasted_iota(jnp.int32, (experts, tokens), 0)
    combine = []
    for k in range(ids_ref.shape[0]):
        hit = ids_ref[k : k + 1, :] == expert
        combine.append(jnp.sum(jnp.where(hit, chosen, 0.0), axis=0, keepdims=True))
    combine_ref[...] = jnp.concatenate(combine, axis=0).astype(BF)


def body(out_grad, gate_weights, expert_ids, w_gate, w_up, w_down, saved_gate, saved_up):
    experts = lax.axis_size("local")
    nodes = lax.axis_size("node")
    tokens, features = out_grad.shape
    top = expert_ids.shape[1]
    units, slots = saved_gate.shape[1:]
    hidden = w_down.shape[1]
    shape = jax.ShapeDtypeStruct
    swap = [(i, i ^ 1) for i in range(nodes)]

    capacity = slots // experts
    rows = layout(features, capacity)[2]
    lanes = -(-features // LANES) * LANES
    ids = expert_ids.T
    send, rank = call(
        functools.partial(dispatch_kernel, capacity),
        (shape((experts * rows, LANES), BF), shape((experts, tokens), F32)),
        ids,
        gate_weights.T,
        out_grad.T,
        plain=True,
        mib=60,
    )
    arrived = lax.all_to_all(
        send.reshape(experts, rows, LANES), "local", split_axis=0, concat_axis=0, tiled=True
    )
    node = lax.axis_index("node")
    depth = nodes // 2
    weights = call(
        weights_kernel,
        shape((2, hidden // 2, features), BF),
        jnp.stack([node % 2, node // 2]).astype(jnp.int32),
        w_down[0].T,
        smem=1,
        scratch=[pltpu.VMEM((2, hidden // LANES, 64, features), F32)],
    )
    rounded = -(-slots // LANES) * LANES
    other, packed, slot_gate = call(
        functools.partial(other_half_kernel, capacity),
        (shape((hidden // 2, rounded), BF), shape((slots, lanes), BF), shape((8, slots), F32)),
        arrived.reshape(experts * rows, LANES),
        weights,
    )
    partner = lax.ppermute(other, "node", swap)
    far, relay = depth // 2, depth // 4
    wide = {0: F32, relay: F32, depth - relay: F32}
    blocks = call(
        own_half_kernel,
        [shape((units // 2 if i in (far, depth) else units, rounded), wide.get(i, BF)) for i in range(depth + 1)],
        packed,
        weights,
        partner,
    )

    def send(value, step):
        return lax.ppermute(value, "node", [(n, (n + 2 * step) % nodes) for n in range(nodes)])

    low, high = send(blocks[far], relay), send(blocks[depth], -relay)
    parts = [blocks[0]]
    for step in range(far - 1, 0, -1):
        if step != relay:
            parts += [send(blocks[step], step), send(blocks[depth - step], -step)]
    up, down = call(
        relay_kernel,
        [shape((units, rounded), BF)] * 2,
        blocks[relay],
        blocks[depth - relay],
        low,
        high,
    )
    parts += [send(up, relay), send(down, -relay)]
    piece = call(
        hidden_kernel,
        shape((2 * units + EXTRA, slots), BF),
        saved_gate[0],
        saved_up[0],
        slot_gate,
        *parts,
    )
    gathered = lax.all_gather(piece, "node", axis=0, tiled=False)
    back = call(
        functools.partial(input_kernel, capacity),
        shape((experts * rows, LANES), BF),
        gathered,
        w_gate[0],
        w_up[0],
        scratch=[pltpu.VMEM((lanes, rounded), F32), pltpu.VMEM((rounded, lanes), F32)],
    )
    returned = lax.all_to_all(
        back.reshape(experts, rows, LANES), "local", split_axis=0, concat_axis=0, tiled=True
    )
    grad, combine = call(
        functools.partial(collect_kernel, capacity),
        (shape((features, tokens), BF), shape((top, tokens), BF)),
        returned.reshape(experts * rows, LANES),
        rank,
        ids,
    )
    return grad.T, combine.T


def solution(mesh):
    in_specs = (
        P("local", "node"),
        P("local", None),
        P("local", None),
        P("local", "node", None),
        P("local", "node", None),
        P("local", None, "node"),
        P("local", "node", None),
        P("local", "node", None),
    )
    out_specs = (P("local", "node"), P("local", None))
    return jax.shard_map(body, mesh=mesh, in_specs=in_specs, out_specs=out_specs, check_vma=False)
```

```python
import functools

import jax
import jax.numpy as jnp
from jax import lax
from jax.experimental import pallas as pl
from jax.experimental.pallas import tpu as pltpu
from jax.sharding import PartitionSpec as P

BF = jnp.bfloat16
F32 = jnp.float32
LANES = 128
GROUP = 8
EXTRA = 16


def call(kernel, outs, *operands, smem=0, scratch=(), plain=False, mib=32):
    vmem = pl.BlockSpec() if plain else pl.BlockSpec(memory_space=pltpu.VMEM)
    spec = [pl.BlockSpec(memory_space=pltpu.SMEM)] * smem
    spec += [vmem] * (len(operands) - smem)
    return pl.pallas_call(
        kernel,
        out_shape=outs,
        in_specs=spec,
        out_specs=jax.tree.map(lambda _: vmem, outs),
        scratch_shapes=list(scratch),
        compiler_params=pltpu.CompilerParams(vmem_limit_bytes=mib * 2**20),
    )(*operands)


def dot(a, b, dims):
    return lax.dot_general(a, b, (dims, ((), ())), preferred_element_type=F32)


NN = ((1,), (0,))
NT = ((1,), (1,))


def layout(features, capacity):
    full = features // LANES
    scalars = full * capacity + (capacity + 1) // 2
    return full, scalars, -(-(scalars + 1) // 16) * 16


def place_codes(features, capacity):
    full, scalars, rows = layout(features, capacity)
    q = lax.broadcasted_iota(jnp.int32, (rows, LANES), 0)
    codes = []
    for c in range(full):
        at = q - c * capacity
        codes.append(jnp.where((at >= 0) & (at < capacity), at, -2))
    at = 2 * (q - full * capacity)
    tail = (at >= 0) & (q < scalars)
    codes.append(jnp.where(tail, at, -2))
    codes.append(jnp.where(tail & (at + 1 < capacity), at + 1, -2))
    return [code.astype(F32).astype(BF) for code in codes]


def picks(rank, features, capacity):
    experts, tokens = rank.shape
    one, zero = jnp.ones((), BF), jnp.zeros((), BF)
    place = rank.astype(BF)[:, None, :]
    out = []
    for code in place_codes(features, capacity):
        hit = jnp.where(place == code[None], one, zero)
        out.append(hit.reshape(experts * code.shape[0], tokens))
    return out


def slot_diagonal(height):
    j = lax.broadcasted_iota(jnp.int32, (1, height, LANES), 1)
    lane = lax.broadcasted_iota(jnp.int32, (1, height, LANES), 2)
    return jnp.where(j == lane, 1.0, 0.0).astype(F32)


def slot_of_row(shape, dim, capacity):
    r = lax.broadcasted_iota(jnp.int32, shape, dim)
    source = jnp.zeros(shape, jnp.int32)
    for s in range(1, GROUP):
        source += jnp.where(r >= s * capacity, 1, 0)
    return source, r - source * capacity


def packing(features, capacity, rows_first):
    full, scalars, rows = layout(features, capacity)
    tight, wide = GROUP * capacity, GROUP * rows
    shape = (wide, tight) if rows_first else (tight, wide)
    source, slot = slot_of_row(shape, 1 if rows_first else 0, capacity)
    at = lax.broadcasted_iota(jnp.int32, shape, 0 if rows_first else 1) - source * rows
    targets = [slot + c * capacity for c in range(full)]
    targets += [lax.shift_right_logical(slot, 1) + full * capacity, scalars]
    return [jnp.where(at == target, 1.0, 0.0).astype(BF) for target in targets]


def odd(slot):
    return (slot & 1) == 1


def dispatch_kernel(capacity, ids_ref, gates_ref, grad_ref, send_ref, rank_ref):
    experts, tokens = rank_ref.shape
    features = grad_ref.shape[0]
    full, scalars, rows = layout(features, capacity)
    expert = lax.broadcasted_iota(jnp.int32, (experts, tokens), 0)
    mask = jnp.zeros((experts, tokens), F32)
    weight = jnp.zeros((experts, tokens), F32)
    for k in range(ids_ref.shape[0]):
        hit = ids_ref[k : k + 1, :] == expert
        mask = jnp.where(hit, 1.0, mask)
        weight = jnp.where(hit, gates_ref[k : k + 1, :].astype(F32), weight)
    earlier = lax.broadcasted_iota(jnp.int32, (tokens, tokens), 0) < lax.broadcasted_iota(
        jnp.int32, (tokens, tokens), 1
    )
    rank = dot(mask.astype(BF), jnp.where(earlier, 1.0, 0.0).astype(BF), NN)
    rank = jnp.where(mask > 0.0, rank, -1.0)
    rank_ref[...] = rank
    height = -(-capacity // 8) * 8
    j = lax.broadcasted_iota(jnp.int32, (experts, height, tokens), 1).astype(F32)
    gate = jnp.where(rank[:, None, :] == j, weight[:, None, :], 0.0)
    gate = jnp.sum(gate, axis=2, keepdims=True)
    gate = jnp.sum(gate * slot_diagonal(height), axis=1, keepdims=True)
    tail = grad_ref[full * LANES :, :]
    empty = jnp.zeros((LANES - tail.shape[0], tokens), BF)
    pieces = [grad_ref[c * LANES : (c + 1) * LANES, :] for c in range(full)]
    pieces += [jnp.concatenate([tail, empty], axis=0), jnp.concatenate([empty, tail], axis=0)]
    total = dot(
        jnp.concatenate(picks(rank, features, capacity), axis=1),
        jnp.concatenate(pieces, axis=1),
        NT,
    )
    q = lax.broadcasted_iota(jnp.int32, (experts, rows, LANES), 1)
    total = jnp.where(q == scalars, gate, total.reshape(experts, rows, LANES))
    send_ref[...] = total.reshape(experts * rows, LANES).astype(BF)


def weights_kernel(place_ref, down_ref, out_ref, rows_ref):
    core, start = place_ref[0], place_ref[1]
    features, hidden = down_ref.shape
    blocks = hidden // LANES
    rows = down_ref[...].astype(F32).T.reshape(blocks, LANES, features)
    low, high = rows[:, :64], rows[:, 64:]
    rows_ref[0] = jnp.where(core == 0, low, high)
    rows_ref[1] = jnp.where(core == 0, high, low)
    for step in range(blocks):
        block = lax.rem(start + step, blocks)
        for half in range(2):
            out_ref[half, step * 64 : (step + 1) * 64, :] = rows_ref[half, block].astype(BF)


def other_half_kernel(capacity, arrived_ref, weight_ref, out_ref, rows_ref, gate_ref):
    features = weight_ref.shape[2]
    full, _, rows = layout(features, capacity)
    tight, wide = GROUP * capacity, GROUP * rows
    groups = arrived_ref.shape[0] // wide
    packs = packing(features, capacity, False)
    _, slot = slot_of_row((tight, LANES), 0, capacity)
    lane = lax.broadcasted_iota(jnp.int32, (tight, LANES), 1)
    for g in range(0, groups, 2):
        pair = jnp.concatenate(
            [arrived_ref[h * wide : (h + 1) * wide, :] for h in (g, g + 1)], axis=1
        )
        at = slice(g * tight, (g + 2) * tight)
        got = [dot(pack, pair, NN) for pack in packs]
        for c in range(full + 1):
            halves = []
            for h in range(2):
                piece = got[c][:, h * LANES : (h + 1) * LANES]
                if c == full:
                    gates = got[full + 1][:, h * LANES : (h + 1) * LANES]
                    gate = jnp.sum(jnp.where(lane == slot, gates, 0.0), axis=1, keepdims=True)
                    piece = jnp.where(odd(slot), pltpu.roll(piece, 64, 1), piece)
                    piece = jnp.where(lane < 64, piece, gate)
                halves.append(piece)
            rows_ref[at, c * LANES : (c + 1) * LANES] = jnp.concatenate(halves, axis=0).astype(BF)
    slots = rows_ref.shape[0]
    out_ref[:, :slots] = dot(weight_ref[1], rows_ref[:, :features], NT).astype(BF)
    if out_ref.shape[1] > slots:
        out_ref[:, slots:] = jnp.zeros((out_ref.shape[0], out_ref.shape[1] - slots), BF)
    lane = lax.broadcasted_iota(jnp.int32, (8, LANES), 1)
    at = jnp.where(lane == 64, 1.0, 0.0).astype(BF)
    gate_ref[...] = dot(at, rows_ref[:, full * LANES :], NT)


def own_half_kernel(rows_ref, weight_ref, partner_ref, *out_refs):
    features = weight_ref.shape[2]
    slots = rows_ref.shape[0]
    units = out_refs[0].shape[0]
    total = dot(weight_ref[0], rows_ref[:, :features], NT) + partner_ref[:, :slots].astype(F32)
    for step, out_ref in enumerate(out_refs):
        out_ref[:, :slots] = total[step * units : (step + 1) * units].astype(out_ref.dtype)
        if out_ref.shape[1] > slots:
            out_ref[:, slots:] = jnp.zeros((units, out_ref.shape[1] - slots), out_ref.dtype)


def hidden_kernel(gate_ref, up_ref, slot_gate_ref, *refs):
    *parts, out_ref = refs
    slots = gate_ref.shape[1]
    raw = parts[0][:, :slots].astype(F32)
    for part in parts[1:]:
        raw += part[:, :slots].astype(F32)
    g = gate_ref[...].astype(F32)
    u = up_ref[...].astype(F32)
    sigma = 1.0 / (1.0 + jnp.exp(-g))
    activ = g * sigma
    slope = sigma * (1.0 + g * (1.0 - sigma))
    combine = jnp.sum(raw * activ * u, axis=0, keepdims=True)
    scaled = raw * slot_gate_ref[0:1, :]
    units = g.shape[0]
    out_ref[:units, :] = (scaled * u * slope).astype(BF)
    out_ref[units : 2 * units, :] = (scaled * activ).astype(BF)
    high = combine.astype(BF).astype(F32)
    row = lax.broadcasted_iota(jnp.int32, (EXTRA, g.shape[1]), 0)
    extra = jnp.where(row == 0, high, jnp.where(row == 1, combine - high, 0.0))
    out_ref[2 * units :, :] = extra.astype(BF)


def input_kernel(capacity, all_ref, gate_ref, up_ref, out_ref, wide_ref, rows_ref):
    nodes, height, slots = all_ref.shape
    units = (height - EXTRA) // 2
    features = gate_ref.shape[0]
    gate_pre = all_ref[:, :units, :].reshape(nodes * units, slots)
    up_pre = all_ref[:, units : 2 * units, :].reshape(nodes * units, slots)
    wide_ref[:features, :slots] = dot(gate_ref[...], gate_pre, NN) + dot(up_ref[...], up_pre, NN)
    extra = all_ref[0, 2 * units :, :].astype(F32)
    for n in range(1, nodes):
        extra += all_ref[n, 2 * units :, :].astype(F32)
    spare = wide_ref.shape[0] - features
    wide_ref[features:, :slots] = jnp.broadcast_to(extra[0:1] + extra[1:2], (spare, slots))
    beyond = wide_ref.shape[1] - slots
    if beyond:
        wide_ref[:, slots:] = jnp.zeros((wide_ref.shape[0], beyond), F32)
    rows_ref[...] = wide_ref[...].T
    full, _, rows = layout(features, capacity)
    tight, wide = GROUP * capacity, GROUP * rows
    groups = slots // tight
    packs = packing(features, capacity, True)
    _, slot = slot_of_row((tight, LANES), 0, capacity)
    lane = lax.broadcasted_iota(jnp.int32, (tight, LANES), 1)
    for g in range(0, groups, 2):
        pieces = []
        for h in (g, g + 1):
            at = slice(h * tight, (h + 1) * tight)
            mine = [rows_ref[at, c * LANES : (c + 1) * LANES] for c in range(full + 1)]
            tail = mine.pop()
            turned = pltpu.roll(tail, 64, 1)
            mine.append(jnp.where((lane >= 64) == odd(slot), jnp.where(odd(slot), turned, tail), 0.0))
            scalar = jnp.where(lane < 64, turned, tail)
            mine.append(jnp.where(lane == slot, scalar, 0.0))
            pieces.append([piece.astype(BF) for piece in mine])
        total = jnp.zeros((wide, 2 * LANES), F32)
        for pack, low, high in zip(packs, *pieces):
            total += dot(pack, jnp.concatenate([low, high], axis=1), NN)
        for h in range(2):
            out_ref[(g + h) * wide : (g + h + 1) * wide, :] = total[
                :, h * LANES : (h + 1) * LANES
            ].astype(BF)


def collect_kernel(capacity, back_ref, rank_ref, ids_ref, grad_ref, combine_ref):
    experts, tokens = rank_ref.shape
    features = grad_ref.shape[0]
    full, scalars, rows = layout(features, capacity)
    rank = rank_ref[...]
    values = back_ref[...].astype(F32)
    turned = values.T.astype(BF)
    sums = [dot(turned, pick, NN) for pick in picks(rank, features, capacity)]
    for c in range(full):
        grad_ref[c * LANES : (c + 1) * LANES, :] = sums[c].astype(BF)
    grad_ref[full * LANES :, :] = (sums[full][:64] + sums[full + 1][64:]).astype(BF)
    height = -(-capacity // 8) * 8
    carried = values.reshape(experts, rows, LANES)[:, scalars : scalars + 1, :]
    column = jnp.sum(carried * slot_diagonal(height), axis=2, keepdims=True)
    j = lax.broadcasted_iota(jnp.int32, (experts, height, tokens), 1).astype(F32)
    chosen = jnp.sum(jnp.where(rank[:, None, :] == j, column, 0.0), axis=1)
    expert = lax.broadcasted_iota(jnp.int32, (experts, tokens), 0)
    combine = []
    for k in range(ids_ref.shape[0]):
        hit = ids_ref[k : k + 1, :] == expert
        combine.append(jnp.sum(jnp.where(hit, chosen, 0.0), axis=0, keepdims=True))
    combine_ref[...] = jnp.concatenate(combine, axis=0).astype(BF)


def body(out_grad, gate_weights, expert_ids, w_gate, w_up, w_down, saved_gate, saved_up):
    experts = lax.axis_size("local")
    nodes = lax.axis_size("node")
    tokens, features = out_grad.shape
    top = expert_ids.shape[1]
    units, slots = saved_gate.shape[1:]
    hidden = w_down.shape[1]
    shape = jax.ShapeDtypeStruct
    swap = [(i, i ^ 1) for i in range(nodes)]

    capacity = slots // experts
    rows = layout(features, capacity)[2]
    lanes = -(-features // LANES) * LANES
    ids = expert_ids.T
    send, rank = call(
        functools.partial(dispatch_kernel, capacity),
        (shape((experts * rows, LANES), BF), shape((experts, tokens), F32)),
        ids,
        gate_weights.T,
        out_grad.T,
        plain=True,
        mib=60,
    )
    arrived = lax.all_to_all(
        send.reshape(experts, rows, LANES), "local", split_axis=0, concat_axis=0, tiled=True
    )
    node = lax.axis_index("node")
    weights = call(
        weights_kernel,
        shape((2, hidden // 2, features), BF),
        jnp.stack([node % 2, node // 2]).astype(jnp.int32),
        w_down[0].T,
        smem=1,
        scratch=[pltpu.VMEM((2, hidden // LANES, 64, features), F32)],
    )
    rounded = -(-slots // LANES) * LANES
    other, packed, slot_gate = call(
        functools.partial(other_half_kernel, capacity),
        (shape((hidden // 2, rounded), BF), shape((slots, lanes), BF), shape((8, slots), F32)),
        arrived.reshape(experts * rows, LANES),
        weights,
    )
    depth = nodes // 2
    own, *others = call(
        own_half_kernel,
        [shape((units, rounded), BF if step else F32) for step in range(depth)],
        packed,
        weights,
        lax.ppermute(other, "node", swap),
    )
    parts = [own]
    for step in sorted(range(1, depth), key=lambda step: -min(step, depth - step)):
        onward = [(n, (n + 2 * step) % nodes) for n in range(nodes)]
        parts.append(lax.ppermute(others[step - 1], "node", onward))
    piece = call(
        hidden_kernel,
        shape((2 * units + EXTRA, slots), BF),
        saved_gate[0],
        saved_up[0],
        slot_gate,
        *parts,
    )
    gathered = lax.all_gather(piece, "node", axis=0, tiled=False)
    back = call(
        functools.partial(input_kernel, capacity),
        shape((experts * rows, LANES), BF),
        gathered,
        w_gate[0],
        w_up[0],
        scratch=[pltpu.VMEM((lanes, rounded), F32), pltpu.VMEM((rounded, lanes), F32)],
    )
    returned = lax.all_to_all(
        back.reshape(experts, rows, LANES), "local", split_axis=0, concat_axis=0, tiled=True
    )
    grad, combine = call(
        functools.partial(collect_kernel, capacity),
        (shape((features, tokens), BF), shape((top, tokens), BF)),
        returned.reshape(experts * rows, LANES),
        rank,
        ids,
    )
    return grad.T, combine.T


def solution(mesh):
    in_specs = (
        P("local", "node"),
        P("local", None),
        P("local", None),
        P("local", "node", None),
        P("local", "node", None),
        P("local", None, "node"),
        P("local", "node", None),
        P("local", "node", None),
    )
    out_specs = (P("local", "node"), P("local", None))
    return jax.shard_map(body, mesh=mesh, in_specs=in_specs, out_specs=out_specs, check_vma=False)
```

```python
import functools

import jax
import jax.numpy as jnp
from jax import lax
from jax.experimental import pallas as pl
from jax.experimental.pallas import tpu as pltpu
from jax.sharding import PartitionSpec as P

BF = jnp.bfloat16
F32 = jnp.float32
LANES = 128
GROUP = 8
EXTRA = 16


def call(kernel, outs, *operands, smem=0, scratch=(), plain=False, mib=32):
    vmem = pl.BlockSpec() if plain else pl.BlockSpec(memory_space=pltpu.VMEM)
    spec = [pl.BlockSpec(memory_space=pltpu.SMEM)] * smem
    spec += [vmem] * (len(operands) - smem)
    return pl.pallas_call(
        kernel,
        out_shape=outs,
        in_specs=spec,
        out_specs=jax.tree.map(lambda _: vmem, outs),
        scratch_shapes=list(scratch),
        compiler_params=pltpu.CompilerParams(vmem_limit_bytes=mib * 2**20),
    )(*operands)


def dot(a, b, dims):
    return lax.dot_general(a, b, (dims, ((), ())), preferred_element_type=F32)


NN = ((1,), (0,))
NT = ((1,), (1,))


def layout(features, capacity):
    full = features // LANES
    scalars = full * capacity + (capacity + 1) // 2
    return full, scalars, -(-(scalars + 1) // 16) * 16


def place_codes(features, capacity):
    full, scalars, rows = layout(features, capacity)
    q = lax.broadcasted_iota(jnp.int32, (rows, LANES), 0)
    codes = []
    for c in range(full):
        at = q - c * capacity
        codes.append(jnp.where((at >= 0) & (at < capacity), at, -2))
    at = 2 * (q - full * capacity)
    tail = (at >= 0) & (q < scalars)
    codes.append(jnp.where(tail, at, -2))
    codes.append(jnp.where(tail & (at + 1 < capacity), at + 1, -2))
    return [code.astype(F32).astype(BF) for code in codes]


def picks(rank, features, capacity):
    experts, tokens = rank.shape
    one, zero = jnp.ones((), BF), jnp.zeros((), BF)
    place = rank.astype(BF)[:, None, :]
    out = []
    for code in place_codes(features, capacity):
        hit = jnp.where(place == code[None], one, zero)
        out.append(hit.reshape(experts * code.shape[0], tokens))
    return out


def slot_diagonal(height):
    j = lax.broadcasted_iota(jnp.int32, (1, height, LANES), 1)
    lane = lax.broadcasted_iota(jnp.int32, (1, height, LANES), 2)
    return jnp.where(j == lane, 1.0, 0.0).astype(F32)


def slot_of_row(shape, dim, capacity):
    r = lax.broadcasted_iota(jnp.int32, shape, dim)
    source = jnp.zeros(shape, jnp.int32)
    for s in range(1, GROUP):
        source += jnp.where(r >= s * capacity, 1, 0)
    return source, r - source * capacity


def packing(features, capacity, rows_first):
    full, scalars, rows = layout(features, capacity)
    tight, wide = GROUP * capacity, GROUP * rows
    shape = (wide, tight) if rows_first else (tight, wide)
    source, slot = slot_of_row(shape, 1 if rows_first else 0, capacity)
    at = lax.broadcasted_iota(jnp.int32, shape, 0 if rows_first else 1) - source * rows
    targets = [slot + c * capacity for c in range(full)]
    targets += [lax.shift_right_logical(slot, 1) + full * capacity, scalars]
    return [jnp.where(at == target, 1.0, 0.0).astype(BF) for target in targets]


def odd(slot):
    return (slot & 1) == 1


def dispatch_kernel(capacity, ids_ref, gates_ref, grad_ref, send_ref, rank_ref):
    experts, tokens = rank_ref.shape
    features = grad_ref.shape[0]
    full, scalars, rows = layout(features, capacity)
    expert = lax.broadcasted_iota(jnp.int32, (experts, tokens), 0)
    mask = jnp.zeros((experts, tokens), F32)
    weight = jnp.zeros((experts, tokens), F32)
    for k in range(ids_ref.shape[0]):
        hit = ids_ref[k : k + 1, :] == expert
        mask = jnp.where(hit, 1.0, mask)
        weight = jnp.where(hit, gates_ref[k : k + 1, :].astype(F32), weight)
    earlier = lax.broadcasted_iota(jnp.int32, (tokens, tokens), 0) < lax.broadcasted_iota(
        jnp.int32, (tokens, tokens), 1
    )
    rank = dot(mask.astype(BF), jnp.where(earlier, 1.0, 0.0).astype(BF), NN)
    rank = jnp.where(mask > 0.0, rank, -1.0)
    rank_ref[...] = rank
    height = -(-capacity // 8) * 8
    j = lax.broadcasted_iota(jnp.int32, (experts, height, tokens), 1).astype(F32)
    gate = jnp.where(rank[:, None, :] == j, weight[:, None, :], 0.0)
    gate = jnp.sum(gate, axis=2, keepdims=True)
    gate = jnp.sum(gate * slot_diagonal(height), axis=1, keepdims=True)
    tail = grad_ref[full * LANES :, :]
    empty = jnp.zeros((LANES - tail.shape[0], tokens), BF)
    pieces = [grad_ref[c * LANES : (c + 1) * LANES, :] for c in range(full)]
    pieces += [jnp.concatenate([tail, empty], axis=0), jnp.concatenate([empty, tail], axis=0)]
    total = dot(
        jnp.concatenate(picks(rank, features, capacity), axis=1),
        jnp.concatenate(pieces, axis=1),
        NT,
    )
    q = lax.broadcasted_iota(jnp.int32, (experts, rows, LANES), 1)
    total = jnp.where(q == scalars, gate, total.reshape(experts, rows, LANES))
    send_ref[...] = total.reshape(experts * rows, LANES).astype(BF)


def weights_kernel(place_ref, down_ref, out_ref, rows_ref):
    core, start = place_ref[0], place_ref[1]
    features, hidden = down_ref.shape
    blocks = hidden // LANES
    rows = down_ref[...].astype(F32).T.reshape(blocks, LANES, features)
    low, high = rows[:, :64], rows[:, 64:]
    rows_ref[0] = jnp.where(core == 0, low, high)
    rows_ref[1] = jnp.where(core == 0, high, low)
    for step in range(blocks):
        block = lax.rem(start + step, blocks)
        for half in range(2):
            out_ref[half, step * 64 : (step + 1) * 64, :] = rows_ref[half, block].astype(BF)


def other_half_kernel(capacity, arrived_ref, weight_ref, out_ref, rows_ref, gate_ref):
    features = weight_ref.shape[2]
    full, _, rows = layout(features, capacity)
    tight, wide = GROUP * capacity, GROUP * rows
    groups = arrived_ref.shape[0] // wide
    packs = packing(features, capacity, False)
    _, slot = slot_of_row((tight, LANES), 0, capacity)
    lane = lax.broadcasted_iota(jnp.int32, (tight, LANES), 1)
    for g in range(0, groups, 2):
        pair = jnp.concatenate(
            [arrived_ref[h * wide : (h + 1) * wide, :] for h in (g, g + 1)], axis=1
        )
        at = slice(g * tight, (g + 2) * tight)
        got = [dot(pack, pair, NN) for pack in packs]
        for c in range(full + 1):
            halves = []
            for h in range(2):
                piece = got[c][:, h * LANES : (h + 1) * LANES]
                if c == full:
                    gates = got[full + 1][:, h * LANES : (h + 1) * LANES]
                    gate = jnp.sum(jnp.where(lane == slot, gates, 0.0), axis=1, keepdims=True)
                    piece = jnp.where(odd(slot), pltpu.roll(piece, 64, 1), piece)
                    piece = jnp.where(lane < 64, piece, gate)
                halves.append(piece)
            rows_ref[at, c * LANES : (c + 1) * LANES] = jnp.concatenate(halves, axis=0).astype(BF)
    slots = rows_ref.shape[0]
    out_ref[:, :slots] = dot(weight_ref[1], rows_ref[:, :features], NT).astype(BF)
    if out_ref.shape[1] > slots:
        out_ref[:, slots:] = jnp.zeros((out_ref.shape[0], out_ref.shape[1] - slots), BF)
    lane = lax.broadcasted_iota(jnp.int32, (8, LANES), 1)
    at = jnp.where(lane == 64, 1.0, 0.0).astype(BF)
    gate_ref[...] = dot(at, rows_ref[:, full * LANES :], NT)


def own_half_kernel(rows_ref, weight_ref, partner_ref, *out_refs):
    features = weight_ref.shape[2]
    slots = rows_ref.shape[0]
    units = out_refs[0].shape[0]
    total = dot(weight_ref[0], rows_ref[:, :features], NT) + partner_ref[:, :slots].astype(F32)
    for step, out_ref in enumerate(out_refs):
        out_ref[:, :slots] = total[step * units : (step + 1) * units].astype(out_ref.dtype)
        if out_ref.shape[1] > slots:
            out_ref[:, slots:] = jnp.zeros((units, out_ref.shape[1] - slots), out_ref.dtype)


def hidden_kernel(gate_ref, up_ref, slot_gate_ref, *refs):
    *parts, out_ref = refs
    slots = gate_ref.shape[1]
    raw = parts[0][:, :slots].astype(F32)
    for part in parts[1:]:
        raw += part[:, :slots].astype(F32)
    g = gate_ref[...].astype(F32)
    u = up_ref[...].astype(F32)
    sigma = 1.0 / (1.0 + jnp.exp(-g))
    activ = g * sigma
    slope = sigma * (1.0 + g * (1.0 - sigma))
    combine = jnp.sum(raw * activ * u, axis=0, keepdims=True)
    scaled = raw * slot_gate_ref[0:1, :]
    units = g.shape[0]
    out_ref[:units, :] = (scaled * u * slope).astype(BF)
    out_ref[units : 2 * units, :] = (scaled * activ).astype(BF)
    high = combine.astype(BF).astype(F32)
    row = lax.broadcasted_iota(jnp.int32, (EXTRA, g.shape[1]), 0)
    extra = jnp.where(row == 0, high, jnp.where(row == 1, combine - high, 0.0))
    out_ref[2 * units :, :] = extra.astype(BF)


def input_kernel(capacity, all_ref, gate_ref, up_ref, out_ref, wide_ref, rows_ref):
    nodes, height, slots = all_ref.shape
    units = (height - EXTRA) // 2
    features = gate_ref.shape[0]
    gate_pre = all_ref[:, :units, :].reshape(nodes * units, slots)
    up_pre = all_ref[:, units : 2 * units, :].reshape(nodes * units, slots)
    wide_ref[:features, :slots] = dot(gate_ref[...], gate_pre, NN) + dot(up_ref[...], up_pre, NN)
    extra = all_ref[0, 2 * units :, :].astype(F32)
    for n in range(1, nodes):
        extra += all_ref[n, 2 * units :, :].astype(F32)
    spare = wide_ref.shape[0] - features
    wide_ref[features:, :slots] = jnp.broadcast_to(extra[0:1] + extra[1:2], (spare, slots))
    beyond = wide_ref.shape[1] - slots
    if beyond:
        wide_ref[:, slots:] = jnp.zeros((wide_ref.shape[0], beyond), F32)
    rows_ref[...] = wide_ref[...].T
    full, _, rows = layout(features, capacity)
    tight, wide = GROUP * capacity, GROUP * rows
    groups = slots // tight
    packs = packing(features, capacity, True)
    _, slot = slot_of_row((tight, LANES), 0, capacity)
    lane = lax.broadcasted_iota(jnp.int32, (tight, LANES), 1)
    for g in range(0, groups, 2):
        pieces = []
        for h in (g, g + 1):
            at = slice(h * tight, (h + 1) * tight)
            mine = [rows_ref[at, c * LANES : (c + 1) * LANES] for c in range(full + 1)]
            tail = mine.pop()
            turned = pltpu.roll(tail, 64, 1)
            mine.append(jnp.where((lane >= 64) == odd(slot), jnp.where(odd(slot), turned, tail), 0.0))
            scalar = jnp.where(lane < 64, turned, tail)
            mine.append(jnp.where(lane == slot, scalar, 0.0))
            pieces.append([piece.astype(BF) for piece in mine])
        total = jnp.zeros((wide, 2 * LANES), F32)
        for pack, low, high in zip(packs, *pieces):
            total += dot(pack, jnp.concatenate([low, high], axis=1), NN)
        for h in range(2):
            out_ref[(g + h) * wide : (g + h + 1) * wide, :] = total[
                :, h * LANES : (h + 1) * LANES
            ].astype(BF)


def collect_kernel(capacity, back_ref, rank_ref, ids_ref, grad_ref, combine_ref):
    experts, tokens = rank_ref.shape
    features = grad_ref.shape[0]
    full, scalars, rows = layout(features, capacity)
    rank = rank_ref[...]
    values = back_ref[...].astype(F32)
    turned = values.T.astype(BF)
    sums = [dot(turned, pick, NN) for pick in picks(rank, features, capacity)]
    for c in range(full):
        grad_ref[c * LANES : (c + 1) * LANES, :] = sums[c].astype(BF)
    grad_ref[full * LANES :, :] = (sums[full][:64] + sums[full + 1][64:]).astype(BF)
    height = -(-capacity // 8) * 8
    carried = values.reshape(experts, rows, LANES)[:, scalars : scalars + 1, :]
    column = jnp.sum(carried * slot_diagonal(height), axis=2, keepdims=True)
    j = lax.broadcasted_iota(jnp.int32, (experts, height, tokens), 1).astype(F32)
    chosen = jnp.sum(jnp.where(rank[:, None, :] == j, column, 0.0), axis=1)
    expert = lax.broadcasted_iota(jnp.int32, (experts, tokens), 0)
    combine = []
    for k in range(ids_ref.shape[0]):
        hit = ids_ref[k : k + 1, :] == expert
        combine.append(jnp.sum(jnp.where(hit, chosen, 0.0), axis=0, keepdims=True))
    combine_ref[...] = jnp.concatenate(combine, axis=0).astype(BF)


def body(out_grad, gate_weights, expert_ids, w_gate, w_up, w_down, saved_gate, saved_up):
    experts = lax.axis_size("local")
    nodes = lax.axis_size("node")
    tokens, features = out_grad.shape
    top = expert_ids.shape[1]
    units, slots = saved_gate.shape[1:]
    hidden = w_down.shape[1]
    shape = jax.ShapeDtypeStruct
    swap = [(i, i ^ 1) for i in range(nodes)]

    capacity = slots // experts
    rows = layout(features, capacity)[2]
    lanes = -(-features // LANES) * LANES
    ids = expert_ids.T
    send, rank = call(
        functools.partial(dispatch_kernel, capacity),
        (shape((experts * rows, LANES), BF), shape((experts, tokens), F32)),
        ids,
        gate_weights.T,
        out_grad.T,
        plain=True,
        mib=60,
    )
    arrived = lax.all_to_all(
        send.reshape(experts, rows, LANES), "local", split_axis=0, concat_axis=0, tiled=True
    )
    node = lax.axis_index("node")
    weights = call(
        weights_kernel,
        shape((2, hidden // 2, features), BF),
        jnp.stack([node % 2, node // 2]).astype(jnp.int32),
        w_down[0].T,
        smem=1,
        scratch=[pltpu.VMEM((2, hidden // LANES, 64, features), F32)],
    )
    rounded = -(-slots // LANES) * LANES
    other, packed, slot_gate = call(
        functools.partial(other_half_kernel, capacity),
        (shape((hidden // 2, rounded), BF), shape((slots, lanes), BF), shape((8, slots), F32)),
        arrived.reshape(experts * rows, LANES),
        weights,
    )
    depth = nodes // 2
    own, *others = call(
        own_half_kernel,
        [shape((units, rounded), BF if step else F32) for step in range(depth)],
        packed,
        weights,
        lax.ppermute(other, "node", swap),
    )
    parts = [own]
    for step in sorted(range(1, depth), key=lambda step: min(step, depth - step)):
        onward = [(n, (n + 2 * step) % nodes) for n in range(nodes)]
        parts.append(lax.ppermute(others[step - 1], "node", onward))
    piece = call(
        hidden_kernel,
        shape((2 * units + EXTRA, slots), BF),
        saved_gate[0],
        saved_up[0],
        slot_gate,
        *parts,
    )
    gathered = lax.all_gather(piece, "node", axis=0, tiled=False)
    back = call(
        functools.partial(input_kernel, capacity),
        shape((experts * rows, LANES), BF),
        gathered,
        w_gate[0],
        w_up[0],
        scratch=[pltpu.VMEM((lanes, rounded), F32), pltpu.VMEM((rounded, lanes), F32)],
    )
    returned = lax.all_to_all(
        back.reshape(experts, rows, LANES), "local", split_axis=0, concat_axis=0, tiled=True
    )
    grad, combine = call(
        functools.partial(collect_kernel, capacity),
        (shape((features, tokens), BF), shape((top, tokens), BF)),
        returned.reshape(experts * rows, LANES),
        rank,
        ids,
    )
    return grad.T, combine.T


def solution(mesh):
    in_specs = (
        P("local", "node"),
        P("local", None),
        P("local", None),
        P("local", "node", None),
        P("local", "node", None),
        P("local", None, "node"),
        P("local", "node", None),
        P("local", "node", None),
    )
    out_specs = (P("local", "node"), P("local", None))
    return jax.shard_map(body, mesh=mesh, in_specs=in_specs, out_specs=out_specs, check_vma=False)
```
